32 devices in a mesh: jobs: 2 (over x), seq: 16 (over z, y, core).
Axes of the slice: x: 2, y: 2, z: 4, core: 2. Of those that a mesh axis runs over, the one named last changes fastest.
Arguments:
- queries: bfloat16 [1024, 4096], P(('jobs', 'seq')), parts along dimension 0, may hold values from -12 to 12
- keys: bfloat16 [1024, 4096], P(('jobs', 'seq')), parts along dimension 0, may hold values from -6 to 6
- values: bfloat16 [1024, 4096], P(('jobs', 'seq')), parts along dimension 0, may hold values from -6 to 6
- live_counts: int32 [2, 16], P('jobs', 'seq'), parts along dimension 0, may hold values from 4 to 16, as said below
- merge_dest: int32 [2, 1024], P('jobs', 'seq'), parts along dimension 0, may hold values from 0 to 15, as said below
- latents: float32 [2, 1024, 64], P('jobs', 'seq'), parts along dimension 0, may hold values from -6 to 6
- guidance: float32 [2], P('jobs'), parts along dimension 0, may hold values from 3 to 6
- step_index: int32 [2], P('jobs'), parts along dimension 0, may hold values from 0 to 980
- out_weight: bfloat16 [4096, 64], replicated, may hold values from -0.09375 to 0.09375
Outputs:
- denoised: float32 [2, 1024, 64], P('jobs', 'seq'), parts along dimension 0
- merged_next: float32 [2, 256, 64], P('jobs', 'seq'), parts along dimension 0
The draws below stay inside these ranges and needn't reach their ends.
There are 2 independent parts, one for each index of `jobs`. The reference program is written for one: setup_inputs(seed, part) draws one part's arguments, and reference() takes and returns one part's arrays. A program takes and returns all parts, laid end to end along the dimension named above; an argument that names none is the same for every part. Nothing has to cross between parts.
Inputs may be any that keep to these rules, and one draw needn't show every extreme that they name: `live_counts`: in every video some merge group has exactly 16 live slots. `merge_dest`: each token names a slot of its own merge group below that group's live count, and every live slot is named by at least one token.
All inputs are finite; a program needn't handle non-finite values.
Results may differ from the reference program's by a relative error of at most 0.0031.
Values may be sent and summed in bfloat16 or wider, within the bound.
A program may use at most 64 MiB of HBM per device.

```python
import math
import jax
import jax.numpy as jnp
from jax import lax

HEADS = 32
HD = 128
C = 64
HALF = 64
CAP_H = 16
TIMESTEPS = 1000
STRIDE = 20
VIDEOS = 1
WIDTH = 4096
SLOTS = 256
S_TOK = 1024
N_SEQ = 16


def draw_queries(key, part):
    row_total = 2 * N_SEQ * CAP_H
    col_total = VIDEOS * HEADS * HD
    base = jnp.clip(2.0 * jax.random.normal(jax.random.fold_in(key, 1), (row_total, col_total), jnp.float32), -12.0, 12.0)
    return base.astype(jnp.bfloat16)


def draw_keys(key, part):
    row_total = 2 * N_SEQ * CAP_H
    col_total = VIDEOS * HEADS * HD
    base = jnp.clip(jax.random.normal(jax.random.fold_in(key, 2), (row_total, col_total), jnp.float32), -6.0, 6.0)
    return base.astype(jnp.bfloat16)


def merge_plan(key):
    low_count = max(2, CAP_H // 4)
    counts = jax.random.randint(jax.random.fold_in(key, 21), (VIDEOS, N_SEQ), low_count, CAP_H + 1)
    full_group = jax.random.randint(jax.random.fold_in(key, 22), (VIDEOS, 1), 0, N_SEQ)
    counts = jnp.where(jnp.arange(N_SEQ, dtype=jnp.int32)[None, :] == full_group, CAP_H, counts).astype(jnp.int32)
    scores = jax.random.randint(jax.random.fold_in(key, 23), (VIDEOS, N_SEQ, HALF), 0, 2 ** 20) * HALF + jnp.arange(HALF, dtype=jnp.int32)
    order = jnp.argsort(scores, axis=-1)
    ranks = jnp.argsort(order, axis=-1).astype(jnp.int32)
    extra = jax.random.randint(jax.random.fold_in(key, 24), (VIDEOS, N_SEQ, HALF), 0, counts[..., None])
    dest = jnp.where(ranks < counts[..., None], ranks, extra).astype(jnp.int32)
    return (counts, dest.reshape(VIDEOS, N_SEQ * HALF))


def draw_live_counts(key, part):
    counts, dest = merge_plan(key)
    return counts


def draw_merge_dest(key, part):
    counts, dest = merge_plan(key)
    return dest


def block_levels(key, shape, cuts, least, largest):
    loudness, own = 1.0, jax.random.fold_in(key, 6)
    for position, shards_of in cuts:
        draws = jnp.exp(jax.random.uniform(jax.random.fold_in(own, position), (shards_of,), jnp.float32, least / len(cuts), largest / len(cuts)))
        loudness = loudness * jnp.repeat(draws, shape[position] // shards_of).reshape([-1 if axis == position else 1 for axis in range(len(shape))])
    return loudness


def bell_draw(own_key, extent, deviation, most, split=(), held_as=jnp.bfloat16):
    entries = deviation * jax.random.normal(own_key, extent, jnp.float32)
    if split:
        entries = entries * block_levels(own_key, extent, split, -0.22, 0.18)
    return jnp.clip(entries, -most, most).astype(held_as)


def setup_inputs(seed: int = 0, part: int = 0) -> dict:
    streams_of = jax.random.split(jax.random.key(seed), 10)
    part_keys = jax.random.split(jax.random.fold_in(streams_of[9], part), 10)
    return {
        "queries": draw_queries(jax.random.fold_in(jax.random.fold_in(streams_of[9], part), 71), part),
        "keys": draw_keys(jax.random.fold_in(jax.random.fold_in(streams_of[9], part), 71), part),
        "values": bell_draw(part_keys[2], (2 * SLOTS, VIDEOS * WIDTH), 1.0, 6.0, ((0, 16),)),
        "live_counts": draw_live_counts(jax.random.fold_in(jax.random.fold_in(streams_of[9], part), 71), part),
        "merge_dest": draw_merge_dest(jax.random.fold_in(jax.random.fold_in(streams_of[9], part), 71), part),
        "latents": bell_draw(part_keys[5], (VIDEOS, S_TOK, C), 1.0, 6.0, ((1, 16),), jnp.float32),
        "guidance": jnp.clip(jax.random.uniform(part_keys[6], (VIDEOS,), jnp.float32, 3.0, 6.0), 3.0, 6.0),
        "step_index": jax.random.randint(part_keys[7], (VIDEOS,), 0, TIMESTEPS - STRIDE + 1).astype(jnp.int32),
        "out_weight": bell_draw(streams_of[8], (WIDTH, C), WIDTH ** -0.5, 0.09375),
    }


neg_big = -1e+30
shift_value = 5.0

def sigma_of(step_value):
    frac = 1.0 - step_value / TIMESTEPS
    return shift_value * frac / (1.0 + (shift_value - 1.0) * frac)

def softmax_attend(query_rows, key_rows, value_rows, key_live, score_scale):
    scores = jnp.dot(query_rows.astype(jnp.float32), key_rows.astype(jnp.float32).T, preferred_element_type=jnp.float32) * score_scale
    scores = jnp.where(key_live[None, :], scores, neg_big)
    row_top = lax.optimization_barrier(jnp.max(scores, axis=-1, keepdims=True))
    weights = jnp.exp(scores - row_top)
    probabilities = (weights / lax.optimization_barrier(jnp.sum(weights, axis=-1, keepdims=True))).astype(jnp.bfloat16)
    return jnp.dot(probabilities.astype(jnp.float32), value_rows.astype(jnp.float32), preferred_element_type=jnp.float32).astype(jnp.bfloat16)

def reference(queries, keys, values, live_counts, merge_dest, latents, guidance, step_index, out_weight):
    branch_slots = N_SEQ * CAP_H
    item_total = VIDEOS * HEADS
    score_scale = 1.0 / math.sqrt(HD)
    query_grid = queries.reshape(2, branch_slots, item_total, HD)
    key_grid = keys.reshape(2, branch_slots, item_total, HD)
    value_grid = values.reshape(2, branch_slots, item_total, HD)
    count_grid = live_counts.reshape(VIDEOS, 2, N_SEQ // 2).transpose(0, 2, 1)
    live_slots = (jnp.arange(CAP_H, dtype=jnp.int32)[None, None, None, :] < count_grid[..., None]).reshape(VIDEOS, branch_slots)

    def one_item(item_index):
        video_index = item_index // HEADS
        key_live = live_slots[video_index]
        branch_outs = [softmax_attend(query_grid[branch_no, :, item_index], key_grid[branch_no, :, item_index], value_grid[branch_no, :, item_index], key_live, score_scale) for branch_no in range(2)]
        conditioned = branch_outs[0].astype(jnp.float32)
        uncond = branch_outs[1].astype(jnp.float32)
        return (uncond + guidance[video_index] * (conditioned - uncond)).astype(jnp.bfloat16)
    guided = lax.map(one_item, jnp.arange(item_total, dtype=jnp.int32))
    guided = guided.reshape(VIDEOS, HEADS, branch_slots, HD).astype(jnp.float32)
    weight_grid = out_weight.reshape(HEADS, HD, C).astype(jnp.float32)
    merged = jnp.einsum('vhsd,hdc->vsc', guided, weight_grid)
    merged = merged.reshape(VIDEOS, N_SEQ // 2, 2, CAP_H, C).transpose(0, 2, 1, 3, 4).reshape(VIDEOS, N_SEQ, CAP_H, C)
    dest_grid = merge_dest.reshape(VIDEOS, N_SEQ, HALF)
    index_grid = jnp.broadcast_to(dest_grid[..., None], (VIDEOS, N_SEQ, HALF, C)).astype(jnp.int32)
    velocity = jnp.take_along_axis(merged, index_grid, axis=2).reshape(VIDEOS, S_TOK, C)
    step_value = step_index.astype(jnp.float32)
    sigma_now = sigma_of(step_value)
    sigma_next = sigma_of(step_value + float(STRIDE))
    denoised = latents - sigma_now[:, None, None] * velocity
    advanced = latents + (sigma_next - sigma_now)[:, None, None] * velocity
    onehot = (dest_grid[..., None] == jnp.arange(CAP_H, dtype=jnp.int32)).astype(jnp.float32)
    slot_sums = jnp.einsum('vnrj,vnrc->vnjc', onehot, advanced.reshape(VIDEOS, N_SEQ, HALF, C), precision=lax.Precision.HIGHEST)
    slot_tally = lax.optimization_barrier(jnp.sum(onehot, axis=2))
    merged_next = (slot_sums / jnp.maximum(slot_tally, 1.0)[..., None]).reshape(VIDEOS, N_SEQ * CAP_H, C)
    return (denoised, merged_next)
```

```python
import functools
import math

import jax
import jax.numpy as jnp
from jax import lax
from jax.experimental import pallas as pl
from jax.experimental.pallas import tpu as pltpu
from jax.sharding import PartitionSpec as P

HEADS = 32
HD = 128
TIMESTEPS = 1000
STRIDE = 20
NEG_BIG = -1e30
SHIFT = 5.0
MESH = pl.DeviceIdType.MESH


def sigma_of(step_value):
    frac = 1.0 - step_value / TIMESTEPS
    return SHIFT * frac / (1.0 + (SHIFT - 1.0) * frac)


def sweep(first, last, body):
    if last - first <= 16:
        for index in range(first, last):
            body(index)
    else:

        def step(index, carry):
            body(index)
            return carry

        lax.fori_loop(first, last, step, 0)


def kernel(
    n,
    items,
    videos,
    query_hbm,
    key_hbm,
    value_hbm,
    count_hbm,
    dest_hbm,
    latent_hbm,
    guidance_hbm,
    step_hbm,
    weight_hbm,
    denoised_ref,
    merged_ref,
    heads_buf,
    count_own,
    count_buf,
    weight_own,
    weight_twice,
    latent_buf,
    dest_buf,
    count_smem,
    guidance_smem,
    step_smem,
    total,
    stage,
    parts,
    barrier_like_sems,
    small_sems,
    head_recv,
    send_sems,
):
    half = n // 2
    me = lax.axis_index("seq")
    branch = me // half
    rank = me % half
    base = branch * half
    rows = query_hbm.shape[0]
    cap = rows // 2
    keys_total = half * rows
    channels = weight_hbm.shape[1]
    scale = 1.0 / math.sqrt(HD)
    sources = (query_hbm, key_hbm, value_hbm)

    barrier = pltpu.get_barrier_semaphore()

    def greet(p):
        pl.semaphore_signal(
            barrier, inc=1, device_id={"seq": (me + p) % n}, device_id_type=MESH
        )

    sweep(1, n, greet)

    count_copy = pltpu.make_async_copy(count_hbm, count_smem, small_sems.at[0])
    count_copy.start()
    head_row = pl.multiple_of(((rank * items) % HEADS) * HD, HD)
    small_copies = [
        pltpu.make_async_copy(guidance_hbm, guidance_smem, small_sems.at[1]),
        pltpu.make_async_copy(step_hbm, step_smem, small_sems.at[2]),
        pltpu.make_async_copy(
            weight_hbm.at[pl.ds(head_row, items * HD)], weight_own, small_sems.at[3]
        ),
        pltpu.make_async_copy(latent_hbm, latent_buf, small_sems.at[4]),
        pltpu.make_async_copy(dest_hbm, dest_buf, small_sems.at[5]),
    ]
    for copy in small_copies:
        copy.start()
    row_at = pl.multiple_of(rank * rows, rows)
    for item in range(items):
        for which in range(3):
            column = pl.multiple_of((rank * items + item) * HD, HD)
            pltpu.make_async_copy(
                sources[which].at[:, pl.ds(column, HD)],
                heads_buf.at[item, which, pl.ds(row_at, rows)],
                head_recv.at[item],
            ).start()

    count_copy.wait()
    count_own[...] = jnp.full(count_own.shape, count_smem[0, 0], jnp.int32) if videos == 1 else (
        jnp.concatenate(
            [jnp.full((1, 128), count_smem[v, 0], jnp.int32) for v in range(videos)], axis=0
        )
    )
    pltpu.make_async_copy(count_own, count_buf.at[me], barrier_like_sems.at[0]).start()

    pl.semaphore_wait(barrier, n - 1)

    def send_count(p):
        pltpu.make_async_remote_copy(
            src_ref=count_own,
            dst_ref=count_buf.at[me],
            send_sem=send_sems.at[0],
            recv_sem=barrier_like_sems.at[0],
            device_id={"seq": (me + p) % n},
            device_id_type=MESH,
        ).start()

    for item in range(items):

        def send_heads(p):
            peer = (rank + p) % half
            column = pl.multiple_of((peer * items + item) * HD, HD)
            for which in range(3):
                pltpu.make_async_remote_copy(
                    src_ref=sources[which].at[:, pl.ds(column, HD)],
                    dst_ref=heads_buf.at[item, which, pl.ds(row_at, rows)],
                    send_sem=send_sems.at[1],
                    recv_sem=head_recv.at[item],
                    device_id={"seq": base + peer},
                    device_id_type=MESH,
                ).start()

        sweep(1, half, send_heads)
        if item == 0:
            sweep(1, n, send_count)

    for copy in small_copies:
        copy.wait()
    weight_twice[...] = jnp.concatenate([weight_own[...], weight_own[...]], axis=1)
    tokens = latent_buf.shape[1]
    slot_hots = []
    latent_sums = []
    for v in range(videos):
        hot = lax.broadcasted_iota(jnp.int32, (cap, tokens), 0) == dest_buf[pl.ds(v, 1), :]
        hot = hot.astype(jnp.float32)
        slot_hots.append(hot)
        latent_sums.append(
            jnp.dot(
                hot,
                latent_buf[v],
                precision=lax.Precision.HIGHEST,
                preferred_element_type=jnp.float32,
            )
        )

    pltpu.make_async_copy(count_buf, count_buf, barrier_like_sems.at[0]).wait()
    video = (rank * items) // HEADS
    lane = lax.broadcasted_iota(jnp.int32, (1, keys_total), 1)
    group_of = ((lane % rows) // cap) * half + lane // rows
    place_of = lane % cap

    def count_step(m, held):
        row = count_buf[m][0:1]
        for v in range(1, videos):
            row = jnp.where(video == v, count_buf[m][v : v + 1], row)
        wide = jnp.concatenate([row] * (keys_total // 128), axis=1)
        return jnp.where(group_of == m, wide, held)

    held = jnp.zeros((1, keys_total), jnp.int32)
    if n <= 16:
        for m in range(n):
            held = count_step(m, held)
    else:
        held = lax.fori_loop(0, n, count_step, held)
    live = place_of < held

    block = min(keys_total, 256)

    for item in range(items):
        pltpu.make_async_copy(heads_buf.at[item], heads_buf.at[item], head_recv.at[item]).wait()

        def attend(index):
            at = pl.ds(pl.multiple_of(index * block, block), block)
            scores = (
                lax.dot_general(
                    heads_buf[item, 0, at, :],
                    heads_buf[item, 1],
                    (((1,), (1,)), ((), ())),
                    preferred_element_type=jnp.float32,
                )
                * scale
            )
            scores = jnp.where(live, scores, NEG_BIG)
            weights = jnp.exp(scores - jnp.max(scores, axis=-1, keepdims=True))
            inverse = 1.0 / jnp.sum(weights, axis=-1, keepdims=True)
            probs = (weights * inverse).astype(jnp.bfloat16)
            attended = jnp.dot(
                probs, heads_buf[item, 2], preferred_element_type=jnp.float32
            ).astype(jnp.bfloat16)
            term = jnp.dot(
                attended,
                weight_twice[item * HD : (item + 1) * HD, :],
                preferred_element_type=jnp.float32,
            )
            if item == 0:
                total[at, :] = term
            else:
                total[at, :] += term

        if keys_total == block:
            attend(0)
        else:

            def attend_step(index, carry):
                attend(index)
                return carry

            lax.fori_loop(0, keys_total // block, attend_step, 0)

    gain = guidance_smem[0]
    for v in range(1, videos):
        gain = jnp.where(video == v, guidance_smem[v], gain)
    gain = jnp.where(branch == 0, gain, 1.0 - gain)
    both = total[...].reshape(half, 2, 2, cap // 2, 2 * channels)
    left = lax.broadcasted_iota(jnp.int32, (half, 2, cap // 2, 2 * channels), 3) < channels
    stage[...] = jnp.where(left, both[:, :, 0], both[:, :, 1]) * gain

    pltpu.make_async_copy(
        stage.at[rank, branch], parts.at[me], barrier_like_sems.at[1]
    ).start()

    def send_part(p):
        peer = (me + p) % n
        pltpu.make_async_remote_copy(
            src_ref=stage.at[peer % half, peer // half],
            dst_ref=parts.at[me],
            send_sem=send_sems.at[2],
            recv_sem=barrier_like_sems.at[1],
            device_id={"seq": peer},
            device_id_type=MESH,
        ).start()

    sweep(1, n, send_part)
    pltpu.make_async_copy(parts, parts, barrier_like_sems.at[1]).wait()

    span = half // videos
    for v in range(videos):
        summed = jnp.sum(parts[v * span : (v + 1) * span], axis=0) + jnp.sum(
            parts[half + v * span : half + (v + 1) * span], axis=0
        )
        merged = jnp.concatenate([summed[:, :channels], summed[:, channels:]], axis=0)
        velocity = lax.dot_general(
            slot_hots[v],
            merged,
            (((0,), (0,)), ((), ())),
            precision=lax.Precision.HIGHEST,
            preferred_element_type=jnp.float32,
        )
        step_value = jnp.full((1, channels), step_smem[v], jnp.int32).astype(jnp.float32)
        sigma_now = sigma_of(step_value)
        sigma_next = sigma_of(step_value + float(STRIDE))
        denoised_ref[v] = latent_buf[v] - sigma_now * velocity
        tally = jnp.sum(slot_hots[v], axis=1, keepdims=True)
        merged_ref[v] = (
            latent_sums[v] + tally * ((sigma_next - sigma_now) * merged)
        ) / jnp.maximum(tally, 1.0)

    pltpu.make_async_copy(
        count_buf.at[pl.ds(0, n - 1)], count_buf.at[pl.ds(0, n - 1)], send_sems.at[0]
    ).wait()
    sent = heads_buf.at[:, :, pl.ds(0, (half - 1) * rows)]
    pltpu.make_async_copy(sent, sent, send_sems.at[1]).wait()
    pltpu.make_async_copy(
        parts.at[pl.ds(0, n - 1)], parts.at[pl.ds(0, n - 1)], send_sems.at[2]
    ).wait()


def local(
    queries, keys, values, live_counts, merge_dest, latents, guidance, step_index, out_weight
):
    n = lax.axis_size("seq")
    half = n // 2
    rows, columns = queries.shape
    videos, tokens, channels = latents.shape
    items = columns // HD // half
    cap = rows // 2
    anywhere = pl.BlockSpec(memory_space=pl.ANY)
    inside = pl.BlockSpec(memory_space=pltpu.VMEM)
    denoised, merged_next = pl.pallas_call(
        functools.partial(kernel, n, items, videos),
        out_shape=(
            jax.ShapeDtypeStruct((videos, tokens, channels), jnp.float32),
            jax.ShapeDtypeStruct((videos, cap, channels), jnp.float32),
        ),
        in_specs=[anywhere] * 9,
        out_specs=(inside, inside),
        scratch_shapes=[
            pltpu.VMEM((items, 3, half * rows, HD), jnp.bfloat16),
            pltpu.VMEM((videos, 128), jnp.int32),
            pltpu.VMEM((n, videos, 128), jnp.int32),
            pltpu.VMEM((items * HD, channels), jnp.bfloat16),
            pltpu.VMEM((items * HD, 2 * channels), jnp.bfloat16),
            pltpu.VMEM((videos, tokens, channels), jnp.float32),
            pltpu.VMEM((videos, tokens), jnp.int32),
            pltpu.SMEM((videos, 1), jnp.int32),
            pltpu.SMEM((videos,), jnp.float32),
            pltpu.SMEM((videos,), jnp.int32),
            pltpu.VMEM((half * rows, 2 * channels), jnp.float32),
            pltpu.VMEM((half, 2, cap // 2, 2 * channels), jnp.float32),
            pltpu.VMEM((n, cap // 2, 2 * channels), jnp.float32),
            pltpu.SemaphoreType.DMA((2,)),
            pltpu.SemaphoreType.DMA((6,)),
            pltpu.SemaphoreType.DMA((items,)),
            pltpu.SemaphoreType.DMA((3,)),
        ],
        compiler_params=pltpu.CompilerParams(
            collective_id=0, has_side_effects=True, vmem_limit_bytes=48 * 1024 * 1024
        ),
    )(
        queries,
        keys,
        values,
        live_counts,
        merge_dest,
        latents,
        guidance,
        step_index,
        out_weight,
    )
    return denoised, merged_next


def solution(mesh):
    placed = (
        P(("jobs", "seq"), None),
        P(("jobs", "seq"), None),
        P(("jobs", "seq"), None),
        P("jobs", "seq"),
        P("jobs", "seq"),
        P("jobs", "seq", None),
        P("jobs"),
        P("jobs"),
        P(),
    )
    return jax.shard_map(
        local,
        mesh=mesh,
        in_specs=placed,
        out_specs=(P("jobs", "seq", None), P("jobs", "seq", None)),
        check_vma=False,
    )
```

```python
import functools
import math

import jax
import jax.numpy as jnp
from jax import lax
from jax.experimental import pallas as pl
from jax.experimental.pallas import tpu as pltpu
from jax.sharding import PartitionSpec as P

HEADS = 32
HD = 128
TIMESTEPS = 1000
STRIDE = 20
NEG_BIG = -1e30
SHIFT = 5.0
MESH = pl.DeviceIdType.MESH


def sigma_of(step_value):
    frac = 1.0 - step_value / TIMESTEPS
    return SHIFT * frac / (1.0 + (SHIFT - 1.0) * frac)


def sweep(first, last, body):
    if last - first <= 16:
        for index in range(first, last):
            body(index)
    else:

        def step(index, carry):
            body(index)
            return carry

        lax.fori_loop(first, last, step, 0)


def kernel(
    n,
    items,
    videos,
    query_hbm,
    key_hbm,
    value_hbm,
    count_hbm,
    dest_hbm,
    latent_hbm,
    guidance_hbm,
    step_hbm,
    weight_hbm,
    denoised_ref,
    merged_ref,
    heads_buf,
    count_own,
    count_buf,
    weight_twice,
    latent_buf,
    dest_buf,
    count_smem,
    guidance_smem,
    step_smem,
    probs,
    total,
    stage,
    parts,
    part_recv,
    small_sems,
    head_recv,
    send_sems,
):
    half = n // 2
    me = lax.axis_index("seq")
    branch = me // half
    rank = me % half
    base = branch * half
    rows = query_hbm.shape[0]
    cap = rows // 2
    keys_total = half * rows
    channels = weight_hbm.shape[0]
    scale = 1.0 / math.sqrt(HD)
    sources = (query_hbm, key_hbm, value_hbm)

    barrier = pltpu.get_barrier_semaphore()

    def greet(p):
        pl.semaphore_signal(
            barrier, inc=1, device_id={"seq": (me + p) % n}, device_id_type=MESH
        )

    sweep(1, n, greet)

    head_col = pl.multiple_of(((rank * items) % HEADS) * HD, HD)
    weight_own = weight_hbm.at[:, pl.ds(head_col, items * HD)]
    small_copies = [
        pltpu.make_async_copy(weight_own, weight_twice.at[pl.ds(0, channels)], small_sems.at[0]),
        pltpu.make_async_copy(
            weight_own, weight_twice.at[pl.ds(channels, channels)], small_sems.at[1]
        ),
        pltpu.make_async_copy(count_hbm, count_smem, small_sems.at[2]),
        pltpu.make_async_copy(guidance_hbm, guidance_smem, small_sems.at[3]),
        pltpu.make_async_copy(step_hbm, step_smem, small_sems.at[4]),
        pltpu.make_async_copy(latent_hbm, latent_buf, small_sems.at[5]),
        pltpu.make_async_copy(dest_hbm, dest_buf, small_sems.at[6]),
    ]
    for copy in small_copies:
        copy.start()
    row_at = pl.multiple_of(rank * rows, rows)

    def heads_of(which, peer):
        column = pl.multiple_of(peer * (items * HD), items * HD)
        return sources[which].at[:, pl.ds(column, items * HD)]

    for which in range(3):
        pltpu.make_async_copy(
            heads_of(which, rank), heads_buf.at[which, pl.ds(row_at, rows)], head_recv.at[which]
        ).start()

    pl.semaphore_wait(barrier, n - 1)

    for which in range(3):

        def send_heads(p):
            peer = (rank + p) % half
            pltpu.make_async_remote_copy(
                src_ref=heads_of(which, peer),
                dst_ref=heads_buf.at[which, pl.ds(row_at, rows)],
                send_sem=send_sems.at[1],
                recv_sem=head_recv.at[which],
                device_id={"seq": base + peer},
                device_id_type=MESH,
            ).start()

        sweep(1, half, send_heads)

    for copy in small_copies:
        copy.wait()
    count_own[...] = jnp.concatenate(
        [jnp.full((1, 128), count_smem[v, 0], jnp.int32) for v in range(videos)], axis=0
    )
    pltpu.make_async_copy(count_own, count_buf.at[me], part_recv.at[0]).start()

    def send_count(p):
        pltpu.make_async_remote_copy(
            src_ref=count_own,
            dst_ref=count_buf.at[me],
            send_sem=send_sems.at[0],
            recv_sem=part_recv.at[0],
            device_id={"seq": (me + p) % n},
            device_id_type=MESH,
        ).start()

    sweep(1, n, send_count)

    tokens = latent_buf.shape[1]
    slot_hots = []
    latent_sums = []
    for v in range(videos):
        hot = lax.broadcasted_iota(jnp.int32, (cap, tokens), 0) == dest_buf[pl.ds(v, 1), :]
        hot = hot.astype(jnp.float32)
        slot_hots.append(hot)
        latent_sums.append(
            jnp.dot(
                hot,
                latent_buf[v],
                precision=lax.Precision.HIGHEST,
                preferred_element_type=jnp.float32,
            )
        )

    pltpu.make_async_copy(count_buf, count_buf, part_recv.at[0]).wait()
    video = (rank * items) // HEADS
    lane = lax.broadcasted_iota(jnp.int32, (1, keys_total), 1)
    group_of = ((lane % rows) // cap) * half + lane // rows
    place_of = lane % cap

    def count_step(m, held):
        row = count_buf[m][0:1]
        for v in range(1, videos):
            row = jnp.where(video == v, count_buf[m][v : v + 1], row)
        wide = jnp.concatenate([row] * (keys_total // 128), axis=1)
        return jnp.where(group_of == m, wide, held)

    held = jnp.zeros((1, keys_total), jnp.int32)
    if n <= 16:
        for m in range(n):
            held = count_step(m, held)
    else:
        held = lax.fori_loop(0, n, count_step, held)
    live = place_of < held

    block = min(keys_total, 256)

    def by_blocks(body):
        if keys_total == block:
            body(pl.ds(0, block))
        else:

            def step(index, carry):
                body(pl.ds(pl.multiple_of(index * block, block), block))
                return carry

            lax.fori_loop(0, keys_total // block, step, 0)

    def arrived(which):
        pltpu.make_async_copy(
            heads_buf.at[which], heads_buf.at[which], head_recv.at[which]
        ).wait()

    arrived(0)
    arrived(1)

    def weigh(at):
        for item in range(items):
            head = pl.ds(item * HD, HD)
            scores = (
                lax.dot_general(
                    heads_buf[0, at, head],
                    heads_buf[1, :, head],
                    (((1,), (1,)), ((), ())),
                    preferred_element_type=jnp.float32,
                )
                * scale
            )
            scores = jnp.where(live, scores, NEG_BIG)
            weights = jnp.exp(scores - jnp.max(scores, axis=-1, keepdims=True))
            inverse = 1.0 / jnp.sum(weights, axis=-1, keepdims=True)
            probs[item, at, :] = (weights * inverse).astype(jnp.bfloat16)

    by_blocks(weigh)
    arrived(2)

    def project(at):
        attended = jnp.concatenate(
            [
                jnp.dot(
                    probs[item, at, :],
                    heads_buf[2, :, item * HD : (item + 1) * HD],
                    preferred_element_type=jnp.float32,
                ).astype(jnp.bfloat16)
                for item in range(items)
            ],
            axis=1,
        )
        total[at, :] = lax.dot_general(
            attended,
            weight_twice[...],
            (((1,), (1,)), ((), ())),
            preferred_element_type=jnp.float32,
        )

    by_blocks(project)

    gain = guidance_smem[0]
    for v in range(1, videos):
        gain = jnp.where(video == v, guidance_smem[v], gain)
    gain = jnp.where(branch == 0, gain, 1.0 - gain)
    both = total[...].reshape(half, 2, 2, cap // 2, 2 * channels)
    left = lax.broadcasted_iota(jnp.int32, (half, 2, cap // 2, 2 * channels), 3) < channels
    stage[...] = jnp.where(left, both[:, :, 0], both[:, :, 1]) * gain

    pltpu.make_async_copy(
        stage.at[rank, branch], parts.at[me], part_recv.at[1]
    ).start()

    def send_part(p):
        peer = (me + p) % n
        pltpu.make_async_remote_copy(
            src_ref=stage.at[peer % half, peer // half],
            dst_ref=parts.at[me],
            send_sem=send_sems.at[2],
            recv_sem=part_recv.at[1],
            device_id={"seq": peer},
            device_id_type=MESH,
        ).start()

    sweep(1, n, send_part)
    pltpu.make_async_copy(parts, parts, part_recv.at[1]).wait()

    span = half // videos
    for v in range(videos):
        summed = jnp.sum(parts[v * span : (v + 1) * span], axis=0) + jnp.sum(
            parts[half + v * span : half + (v + 1) * span], axis=0
        )
        merged = jnp.concatenate([summed[:, :channels], summed[:, channels:]], axis=0)
        velocity = lax.dot_general(
            slot_hots[v],
            merged,
            (((0,), (0,)), ((), ())),
            precision=lax.Precision.HIGHEST,
            preferred_element_type=jnp.float32,
        )
        step_value = jnp.full((1, channels), step_smem[v], jnp.int32).astype(jnp.float32)
        sigma_now = sigma_of(step_value)
        sigma_next = sigma_of(step_value + float(STRIDE))
        denoised_ref[v] = latent_buf[v] - sigma_now * velocity
        tally = jnp.sum(slot_hots[v], axis=1, keepdims=True)
        merged_ref[v] = (
            latent_sums[v] + tally * ((sigma_next - sigma_now) * merged)
        ) / jnp.maximum(tally, 1.0)

    pltpu.make_async_copy(
        count_buf.at[pl.ds(0, n - 1)], count_buf.at[pl.ds(0, n - 1)], send_sems.at[0]
    ).wait()
    sent = heads_buf.at[:, pl.ds(0, (half - 1) * rows)]
    pltpu.make_async_copy(sent, sent, send_sems.at[1]).wait()
    pltpu.make_async_copy(
        parts.at[pl.ds(0, n - 1)], parts.at[pl.ds(0, n - 1)], send_sems.at[2]
    ).wait()


def local(
    queries, keys, values, live_counts, merge_dest, latents, guidance, step_index, out_weight
):
    n = lax.axis_size("seq")
    half = n // 2
    rows, columns = queries.shape
    videos, tokens, channels = latents.shape
    items = columns // HD // half
    cap = rows // 2
    outside = pl.BlockSpec(memory_space=pltpu.HBM)
    inside = pl.BlockSpec(memory_space=pltpu.VMEM)
    denoised, merged_next = pl.pallas_call(
        functools.partial(kernel, n, items, videos),
        out_shape=(
            jax.ShapeDtypeStruct((videos, tokens, channels), jnp.float32),
            jax.ShapeDtypeStruct((videos, cap, channels), jnp.float32),
        ),
        in_specs=[outside] * 9,
        out_specs=(inside, inside),
        scratch_shapes=[
            pltpu.VMEM((3, half * rows, items * HD), jnp.bfloat16),
            pltpu.VMEM((videos, 128), jnp.int32),
            pltpu.VMEM((n, videos, 128), jnp.int32),
            pltpu.VMEM((2 * channels, items * HD), jnp.bfloat16),
            pltpu.VMEM((videos, tokens, channels), jnp.float32),
            pltpu.VMEM((videos, tokens), jnp.int32),
            pltpu.SMEM((videos, 1), jnp.int32),
            pltpu.SMEM((videos,), jnp.float32),
            pltpu.SMEM((videos,), jnp.int32),
            pltpu.VMEM((items, half * rows, half * rows), jnp.bfloat16),
            pltpu.VMEM((half * rows, 2 * channels), jnp.float32),
            pltpu.VMEM((half, 2, cap // 2, 2 * channels), jnp.float32),
            pltpu.VMEM((n, cap // 2, 2 * channels), jnp.float32),
            pltpu.SemaphoreType.DMA((2,)),
            pltpu.SemaphoreType.DMA((7,)),
            pltpu.SemaphoreType.DMA((3,)),
            pltpu.SemaphoreType.DMA((3,)),
        ],
        compiler_params=pltpu.CompilerParams(
            collective_id=0, has_side_effects=True, vmem_limit_bytes=62 * 1024 * 1024
        ),
    )(
        queries,
        keys,
        values,
        live_counts,
        merge_dest,
        latents,
        guidance,
        step_index,
        out_weight.T,
    )
    return denoised, merged_next


def solution(mesh):
    placed = (
        P(("jobs", "seq"), None),
        P(("jobs", "seq"), None),
        P(("jobs", "seq"), None),
        P("jobs", "seq"),
        P("jobs", "seq"),
        P("jobs", "seq", None),
        P("jobs"),
        P("jobs"),
        P(),
    )
    return jax.shard_map(
        local,
        mesh=mesh,
        in_specs=placed,
        out_specs=(P("jobs", "seq", None), P("jobs", "seq", None)),
        check_vma=False,
    )
```

```python
import functools
import math

import jax
import jax.numpy as jnp
from jax import lax
from jax.experimental import pallas as pl
from jax.experimental.pallas import tpu as pltpu
from jax.sharding import PartitionSpec as P

HEADS = 32
HD = 128
TIMESTEPS = 1000
STRIDE = 20
NEG_BIG = -1e30
SHIFT = 5.0
MESH = pl.DeviceIdType.MESH


def sigma_of(step_value):
    frac = 1.0 - step_value / TIMESTEPS
    return SHIFT * frac / (1.0 + (SHIFT - 1.0) * frac)


def sweep(first, last, body):
    if last - first <= 16:
        for index in range(first, last):
            body(index)
    else:

        def step(index, carry):
            body(index)
            return carry

        lax.fori_loop(first, last, step, 0)


def kernel(
    n,
    items,
    videos,
    query_hbm,
    key_hbm,
    value_hbm,
    dest_ref,
    latent_hbm,
    weight_hbm,
    velocity_ref,
    slot_ref,
    heads_buf,
    count_own,
    count_buf,
    weight_twice,
    latent_buf,
    total,
    stage,
    parts,
    part_recv,
    small_sems,
    head_recv,
    send_sems,
):
    half = n // 2
    me = lax.axis_index("seq")
    branch = me // half
    rank = me % half
    base = branch * half
    rows = query_hbm.shape[0]
    cap = rows // 2
    keys_total = half * rows
    channels = weight_hbm.shape[0]
    scale = 1.0 / math.sqrt(HD)
    sources = (query_hbm, key_hbm, value_hbm)

    barrier = pltpu.get_barrier_semaphore()

    def greet(p):
        pl.semaphore_signal(
            barrier, inc=1, device_id={"seq": (me + p) % n}, device_id_type=MESH
        )

    sweep(1, n, greet)

    head_col = pl.multiple_of(((rank * items) % HEADS) * HD, HD)
    weight_own = weight_hbm.at[:, pl.ds(head_col, items * HD)]
    small_copies = [
        pltpu.make_async_copy(weight_own, weight_twice.at[pl.ds(0, channels)], small_sems.at[0]),
        pltpu.make_async_copy(
            weight_own, weight_twice.at[pl.ds(channels, channels)], small_sems.at[1]
        ),
        pltpu.make_async_copy(latent_hbm, latent_buf, small_sems.at[2]),
    ]
    for copy in small_copies:
        copy.start()
    row_at = pl.multiple_of(rank * rows, rows)

    def heads_of(which, peer, item):
        column = pl.multiple_of((peer * items + item) * HD, HD)
        return sources[which].at[:, pl.ds(column, HD)]

    for item in range(items):
        for which in range(3):
            pltpu.make_async_copy(
                heads_of(which, rank, item),
                heads_buf.at[item, which, pl.ds(row_at, rows)],
                head_recv.at[item],
            ).start()

    pl.semaphore_wait(barrier, n - 1)

    count = jnp.max(dest_ref[...].astype(jnp.float32), axis=1, keepdims=True) + 1.0
    count_own[...] = jnp.broadcast_to(count, count_own.shape).astype(jnp.int32)
    pltpu.make_async_copy(count_own, count_buf.at[me], part_recv.at[0]).start()

    def send_count(p):
        pltpu.make_async_remote_copy(
            src_ref=count_own,
            dst_ref=count_buf.at[me],
            send_sem=send_sems.at[0],
            recv_sem=part_recv.at[0],
            device_id={"seq": (me + p) % n},
            device_id_type=MESH,
        ).start()

    for item in range(items):

        def send_heads(p):
            peer = (rank + p) % half
            for which in range(3):
                pltpu.make_async_remote_copy(
                    src_ref=heads_of(which, peer, item),
                    dst_ref=heads_buf.at[item, which, pl.ds(row_at, rows)],
                    send_sem=send_sems.at[1],
                    recv_sem=head_recv.at[item],
                    device_id={"seq": base + peer},
                    device_id_type=MESH,
                ).start()

        sweep(1, half, send_heads)
        if item == 0:
            sweep(1, n, send_count)

    for copy in small_copies:
        copy.wait()

    tokens = latent_buf.shape[1]
    slot_hots, latent_means, shares = [], [], []
    for v in range(videos):
        hot = lax.broadcasted_iota(jnp.int32, (cap, tokens), 0) == dest_ref[v : v + 1, :]
        hot = hot.astype(jnp.float32)
        latent_sum = jnp.dot(
            hot,
            latent_buf[v],
            precision=lax.Precision.HIGHEST,
            preferred_element_type=jnp.float32,
        )
        tally = jnp.sum(hot, axis=1, keepdims=True)
        inverse = 1.0 / jnp.maximum(tally, 1.0)
        slot_hots.append(hot)
        latent_means.append(latent_sum * inverse)
        shares.append(tally * inverse)

    pltpu.make_async_copy(count_buf, count_buf, part_recv.at[0]).wait()
    video = (rank * items) // HEADS
    lane = lax.broadcasted_iota(jnp.int32, (1, keys_total), 1)
    group_of = ((lane % rows) // cap) * half + lane // rows
    place_of = lane % cap

    def count_step(m, held):
        row = count_buf[m][0:1]
        for v in range(1, videos):
            row = jnp.where(video == v, count_buf[m][v : v + 1], row)
        wide = jnp.concatenate([row] * (keys_total // 128), axis=1)
        return jnp.where(group_of == m, wide, held)

    held = jnp.zeros((1, keys_total), jnp.int32)
    if n <= 16:
        for m in range(n):
            held = count_step(m, held)
    else:
        held = lax.fori_loop(0, n, count_step, held)
    live = place_of < held

    block = min(keys_total, 256)

    def by_blocks(body):
        if keys_total == block:
            body(pl.ds(0, block))
        else:

            def step(index, carry):
                body(pl.ds(pl.multiple_of(index * block, block), block))
                return carry

            lax.fori_loop(0, keys_total // block, step, 0)

    for item in range(items):
        pltpu.make_async_copy(heads_buf.at[item], heads_buf.at[item], head_recv.at[item]).wait()

        def attend(at):
            scores = (
                lax.dot_general(
                    heads_buf[item, 0, at, :],
                    heads_buf[item, 1],
                    (((1,), (1,)), ((), ())),
                    preferred_element_type=jnp.float32,
                )
                * scale
            )
            scores = jnp.where(live, scores, NEG_BIG)
            weights = jnp.exp(scores - jnp.max(scores, axis=-1, keepdims=True))
            inverse = 1.0 / jnp.sum(weights, axis=-1, keepdims=True)
            probs = (weights * inverse).astype(jnp.bfloat16)
            attended = jnp.dot(
                probs, heads_buf[item, 2], preferred_element_type=jnp.float32
            ).astype(jnp.bfloat16)
            term = lax.dot_general(
                attended,
                weight_twice[:, item * HD : (item + 1) * HD],
                (((1,), (1,)), ((), ())),
                preferred_element_type=jnp.float32,
            )
            if item == 0:
                total[at, :] = term
            else:
                total[at, :] += term

        by_blocks(attend)

    both = total[...].reshape(half, 2, 2, cap // 2, 2 * channels)
    left = lax.broadcasted_iota(jnp.int32, (half, 2, cap // 2, 2 * channels), 3) < channels
    stage[...] = jnp.where(left, both[:, :, 0], both[:, :, 1])

    pltpu.make_async_copy(
        stage.at[rank, branch], parts.at[me], part_recv.at[1]
    ).start()

    def send_part(p):
        peer = (me + p) % n
        pltpu.make_async_remote_copy(
            src_ref=stage.at[peer % half, peer // half],
            dst_ref=parts.at[me],
            send_sem=send_sems.at[2],
            recv_sem=part_recv.at[1],
            device_id={"seq": peer},
            device_id_type=MESH,
        ).start()

    sweep(1, n, send_part)
    pltpu.make_async_copy(parts, parts, part_recv.at[1]).wait()

    span = half // videos
    left = lax.broadcasted_iota(jnp.int32, (cap // 2, 2 * channels), 1) < channels
    for v in range(videos):
        cond = jnp.sum(parts[v * span : (v + 1) * span], axis=0)
        uncond = jnp.sum(parts[half + v * span : half + (v + 1) * span], axis=0)
        merged = jnp.concatenate(
            [
                jnp.where(left, cond, pltpu.roll(uncond, channels, 1)),
                jnp.where(left, pltpu.roll(cond, channels, 1), uncond),
            ],
            axis=0,
        )
        velocity = lax.dot_general(
            slot_hots[v],
            merged,
            (((0,), (0,)), ((), ())),
            precision=lax.Precision.HIGHEST,
            preferred_element_type=jnp.float32,
        )
        velocity_ref[0, v] = velocity[:, :channels]
        velocity_ref[1, v] = velocity[:, channels:]
        merged = shares[v] * merged
        slot_ref[0, v] = merged[:, :channels]
        slot_ref[1, v] = merged[:, channels:]
        slot_ref[2, v] = latent_means[v]

    pltpu.make_async_copy(
        count_buf.at[pl.ds(0, n - 1)], count_buf.at[pl.ds(0, n - 1)], send_sems.at[0]
    ).wait()
    sent = heads_buf.at[:, :, pl.ds(0, (half - 1) * rows)]
    pltpu.make_async_copy(sent, sent, send_sems.at[1]).wait()
    pltpu.make_async_copy(
        parts.at[pl.ds(0, n - 1)], parts.at[pl.ds(0, n - 1)], send_sems.at[2]
    ).wait()


def local(
    queries, keys, values, live_counts, merge_dest, latents, guidance, step_index, out_weight
):
    n = lax.axis_size("seq")
    half = n // 2
    rows, columns = queries.shape
    videos, tokens, channels = latents.shape
    items = columns // HD // half
    cap = rows // 2
    outside = pl.BlockSpec(memory_space=pltpu.HBM)
    inside = pl.BlockSpec(memory_space=pltpu.VMEM)
    velocities, slots = pl.pallas_call(
        functools.partial(kernel, n, items, videos),
        out_shape=(
            jax.ShapeDtypeStruct((2, videos, tokens, channels), jnp.float32),
            jax.ShapeDtypeStruct((3, videos, cap, channels), jnp.float32),
        ),
        in_specs=[outside] * 3 + [inside] + [outside] * 2,
        out_specs=(inside, inside),
        scratch_shapes=[
            pltpu.VMEM((items, 3, half * rows, HD), jnp.bfloat16),
            pltpu.VMEM((videos, 128), jnp.int32),
            pltpu.VMEM((n, videos, 128), jnp.int32),
            pltpu.VMEM((2 * channels, items * HD), jnp.bfloat16),
            pltpu.VMEM((videos, tokens, channels), jnp.float32),
            pltpu.VMEM((half * rows, 2 * channels), jnp.float32),
            pltpu.VMEM((half, 2, cap // 2, 2 * channels), jnp.float32),
            pltpu.VMEM((n, cap // 2, 2 * channels), jnp.float32),
            pltpu.SemaphoreType.DMA((2,)),
            pltpu.SemaphoreType.DMA((3,)),
            pltpu.SemaphoreType.DMA((items,)),
            pltpu.SemaphoreType.DMA((3,)),
        ],
        compiler_params=pltpu.CompilerParams(
            collective_id=0, has_side_effects=True, vmem_limit_bytes=62 * 1024 * 1024
        ),
    )(
        queries,
        keys,
        values,
        merge_dest,
        latents,
        out_weight.T,
    )
    step_value = step_index.astype(jnp.float32)
    sigma_now = sigma_of(step_value)
    sigma_next = sigma_of(step_value + float(STRIDE))
    gain = guidance[:, None, None]
    velocity = velocities[1] + gain * (velocities[0] - velocities[1])
    denoised = latents - sigma_now[:, None, None] * velocity
    merged = slots[1] + gain * (slots[0] - slots[1])
    merged_next = slots[2] + (sigma_next - sigma_now)[:, None, None] * merged
    return denoised, merged_next


def solution(mesh):
    placed = (
        P(("jobs", "seq"), None),
        P(("jobs", "seq"), None),
        P(("jobs", "seq"), None),
        P("jobs", "seq"),
        P("jobs", "seq"),
        P("jobs", "seq", None),
        P("jobs"),
        P("jobs"),
        P(),
    )
    return jax.shard_map(
        local,
        mesh=mesh,
        in_specs=placed,
        out_specs=(P("jobs", "seq", None), P("jobs", "seq", None)),
        check_vma=False,
    )
```

```python
import functools
import math

import jax
import jax.numpy as jnp
from jax import lax
from jax.experimental import pallas as pl
from jax.experimental.pallas import tpu as pltpu
from jax.sharding import PartitionSpec as P

HEADS = 32
HD = 128
TIMESTEPS = 1000
STRIDE = 20
NEG_BIG = -1e30
SHIFT = 5.0
MESH = pl.DeviceIdType.MESH


def sigma_of(step_value):
    frac = 1.0 - step_value / TIMESTEPS
    return SHIFT * frac / (1.0 + (SHIFT - 1.0) * frac)


def sweep(first, last, body):
    if last - first <= 16:
        for index in range(first, last):
            body(index)
    else:

        def step(index, carry):
            body(index)
            return carry

        lax.fori_loop(first, last, step, 0)


def kernel(
    n,
    items,
    videos,
    query_hbm,
    key_hbm,
    value_hbm,
    dest_ref,
    latent_hbm,
    weight_hbm,
    velocity_ref,
    slot_ref,
    heads_buf,
    count_own,
    count_buf,
    weight_twice,
    latent_buf,
    total,
    stage,
    parts,
    part_recv,
    small_sems,
    head_recv,
    send_sems,
    vouched,
):
    half = n // 2
    me = lax.axis_index("seq")
    branch = me // half
    rank = me % half
    base = branch * half
    rows = query_hbm.shape[0]
    cap = rows // 2
    keys_total = half * rows
    channels = weight_hbm.shape[0]
    scale = 1.0 / math.sqrt(HD)
    sources = (query_hbm, key_hbm, value_hbm)

    barrier = pltpu.get_barrier_semaphore()

    partner = (me + half) % n

    def greet(p):
        pl.semaphore_signal(
            barrier,
            inc=1,
            device_id={"seq": base + (rank + p) % half},
            device_id_type=MESH,
        )

    sweep(1, half, greet)
    pl.semaphore_signal(barrier, inc=1, device_id={"seq": partner}, device_id_type=MESH)

    head_col = pl.multiple_of(((rank * items) % HEADS) * HD, HD)
    weight_own = weight_hbm.at[:, pl.ds(head_col, items * HD)]
    small_copies = [
        pltpu.make_async_copy(weight_own, weight_twice.at[pl.ds(0, channels)], small_sems.at[0]),
        pltpu.make_async_copy(
            weight_own, weight_twice.at[pl.ds(channels, channels)], small_sems.at[1]
        ),
        pltpu.make_async_copy(latent_hbm, latent_buf, small_sems.at[2]),
    ]
    for copy in small_copies:
        copy.start()
    row_at = pl.multiple_of(rank * rows, rows)

    def heads_of(which, peer, item):
        column = pl.multiple_of((peer * items + item) * HD, HD)
        return sources[which].at[:, pl.ds(column, HD)]

    for item in range(items):
        for which in range(3):
            pltpu.make_async_copy(
                heads_of(which, rank, item),
                heads_buf.at[item, which, pl.ds(row_at, rows)],
                head_recv.at[item],
            ).start()

    pl.semaphore_wait(barrier, half)

    def vouch(p):
        pl.semaphore_signal(
            vouched,
            inc=1,
            device_id={"seq": base + (rank + p) % half},
            device_id_type=MESH,
        )

    sweep(1, half, vouch)

    count = jnp.max(dest_ref[...].astype(jnp.float32), axis=1, keepdims=True) + 1.0
    count_own[...] = jnp.broadcast_to(count, count_own.shape).astype(jnp.int32)
    pltpu.make_async_copy(count_own, count_buf.at[me], part_recv.at[0]).start()

    def send_count(p):
        pltpu.make_async_remote_copy(
            src_ref=count_own,
            dst_ref=count_buf.at[me],
            send_sem=send_sems.at[0],
            recv_sem=part_recv.at[0],
            device_id={"seq": (me + p) % n},
            device_id_type=MESH,
        ).start()

    for item in range(items):

        def send_heads(p):
            peer = (rank + p) % half
            for which in range(3):
                pltpu.make_async_remote_copy(
                    src_ref=heads_of(which, peer, item),
                    dst_ref=heads_buf.at[item, which, pl.ds(row_at, rows)],
                    send_sem=send_sems.at[1],
                    recv_sem=head_recv.at[item],
                    device_id={"seq": base + peer},
                    device_id_type=MESH,
                ).start()

        sweep(1, half, send_heads)

    pl.semaphore_wait(vouched, half - 1)
    sweep(1, n, send_count)

    for copy in small_copies:
        copy.wait()

    tokens = latent_buf.shape[1]
    slot_hots, latent_means, shares = [], [], []
    for v in range(videos):
        hot = lax.broadcasted_iota(jnp.int32, (cap, tokens), 0) == dest_ref[v : v + 1, :]
        hot = hot.astype(jnp.float32)
        latent_sum = jnp.dot(
            hot,
            latent_buf[v],
            precision=lax.Precision.HIGHEST,
            preferred_element_type=jnp.float32,
        )
        tally = jnp.sum(hot, axis=1, keepdims=True)
        inverse = 1.0 / jnp.maximum(tally, 1.0)
        slot_hots.append(hot)
        latent_means.append(latent_sum * inverse)
        shares.append(tally * inverse)

    pltpu.make_async_copy(count_buf, count_buf, part_recv.at[0]).wait()
    video = (rank * items) // HEADS
    lane = lax.broadcasted_iota(jnp.int32, (1, keys_total), 1)
    group_of = ((lane % rows) // cap) * half + lane // rows
    place_of = lane % cap

    def count_step(m, held):
        row = count_buf[m][0:1]
        for v in range(1, videos):
            row = jnp.where(video == v, count_buf[m][v : v + 1], row)
        wide = jnp.concatenate([row] * (keys_total // 128), axis=1)
        return jnp.where(group_of == m, wide, held)

    held = jnp.zeros((1, keys_total), jnp.int32)
    if n <= 16:
        for m in range(n):
            held = count_step(m, held)
    else:
        held = lax.fori_loop(0, n, count_step, held)
    live = place_of < held

    def by_blocks(block, body):
        if keys_total <= 4 * block:
            for index in range(keys_total // block):
                body(index)
        else:

            def step(index, carry):
                body(index)
                return carry

            lax.fori_loop(0, keys_total // block, step, 0)

    left = lax.broadcasted_iota(jnp.int32, (cap // 2, 2 * channels), 1) < channels

    def send_part(of_rank, group, piece):
        owner = group * half + of_rank
        stage[of_rank, group] = jnp.where(left, piece[0], piece[1])

        @pl.when(owner == me)
        def _():
            pltpu.make_async_copy(
                stage.at[of_rank, group], parts.at[me], part_recv.at[1]
            ).start()

        @pl.when(owner != me)
        def _():
            pltpu.make_async_remote_copy(
                src_ref=stage.at[of_rank, group],
                dst_ref=parts.at[me],
                send_sem=send_sems.at[2],
                recv_sem=part_recv.at[1],
                device_id={"seq": owner},
                device_id_type=MESH,
            ).start()

    for item in range(items):
        pltpu.make_async_copy(heads_buf.at[item], heads_buf.at[item], head_recv.at[item]).wait()

        last = item == items - 1
        block = 128 if last else min(keys_total, 256)

        def attend(index):
            at = pl.ds(pl.multiple_of(index * block, block), block)
            scores = (
                lax.dot_general(
                    heads_buf[item, 0, at, :],
                    heads_buf[item, 1],
                    (((1,), (1,)), ((), ())),
                    preferred_element_type=jnp.float32,
                )
                * scale
            )
            scores = jnp.where(live, scores, NEG_BIG)
            weights = jnp.exp(scores - jnp.max(scores, axis=-1, keepdims=True))
            inverse = 1.0 / jnp.sum(weights, axis=-1, keepdims=True)
            probs = (weights * inverse).astype(jnp.bfloat16)
            attended = jnp.dot(
                probs, heads_buf[item, 2], preferred_element_type=jnp.float32
            ).astype(jnp.bfloat16)
            term = lax.dot_general(
                attended,
                weight_twice[:, item * HD : (item + 1) * HD],
                (((1,), (1,)), ((), ())),
                preferred_element_type=jnp.float32,
            )
            if item > 0:
                term = total[at, :] + term
            if not last:
                total[at, :] = term
                return
            ranks = block // rows
            pieces = term.reshape(ranks, 2, 2, cap // 2, 2 * channels)
            for place in range(ranks):
                for group in range(2):
                    send_part(index * ranks + place, group, pieces[place, group])

        by_blocks(block, attend)

    pltpu.make_async_copy(parts, parts, part_recv.at[1]).wait()

    span = half // videos
    for v in range(videos):
        cond = jnp.sum(parts[v * span : (v + 1) * span], axis=0)
        uncond = jnp.sum(parts[half + v * span : half + (v + 1) * span], axis=0)
        merged = jnp.concatenate(
            [
                jnp.where(left, cond, pltpu.roll(uncond, channels, 1)),
                jnp.where(left, pltpu.roll(cond, channels, 1), uncond),
            ],
            axis=0,
        )
        velocity = lax.dot_general(
            slot_hots[v],
            merged,
            (((0,), (0,)), ((), ())),
            precision=lax.Precision.HIGHEST,
            preferred_element_type=jnp.float32,
        )
        velocity_ref[0, v] = velocity[:, :channels]
        velocity_ref[1, v] = velocity[:, channels:]
        merged = shares[v] * merged
        slot_ref[0, v] = merged[:, :channels]
        slot_ref[1, v] = merged[:, channels:]
        slot_ref[2, v] = latent_means[v]

    pltpu.make_async_copy(
        count_buf.at[pl.ds(0, n - 1)], count_buf.at[pl.ds(0, n - 1)], send_sems.at[0]
    ).wait()
    sent = heads_buf.at[:, :, pl.ds(0, (half - 1) * rows)]
    pltpu.make_async_copy(sent, sent, send_sems.at[1]).wait()
    pltpu.make_async_copy(
        parts.at[pl.ds(0, n - 1)], parts.at[pl.ds(0, n - 1)], send_sems.at[2]
    ).wait()


def local(
    queries, keys, values, live_counts, merge_dest, latents, guidance, step_index, out_weight
):
    n = lax.axis_size("seq")
    half = n // 2
    rows, columns = queries.shape
    videos, tokens, channels = latents.shape
    items = columns // HD // half
    cap = rows // 2
    outside = pl.BlockSpec(memory_space=pltpu.HBM)
    inside = pl.BlockSpec(memory_space=pltpu.VMEM)
    velocities, slots = pl.pallas_call(
        functools.partial(kernel, n, items, videos),
        out_shape=(
            jax.ShapeDtypeStruct((2, videos, tokens, channels), jnp.float32),
            jax.ShapeDtypeStruct((3, videos, cap, channels), jnp.float32),
        ),
        in_specs=[outside] * 3 + [inside] + [outside] * 2,
        out_specs=(inside, inside),
        scratch_shapes=[
            pltpu.VMEM((items, 3, half * rows, HD), jnp.bfloat16),
            pltpu.VMEM((videos, 128), jnp.int32),
            pltpu.VMEM((n, videos, 128), jnp.int32),
            pltpu.VMEM((2 * channels, items * HD), jnp.bfloat16),
            pltpu.VMEM((videos, tokens, channels), jnp.float32),
            pltpu.VMEM((half * rows, 2 * channels), jnp.float32),
            pltpu.VMEM((half, 2, cap // 2, 2 * channels), jnp.float32),
            pltpu.VMEM((n, cap // 2, 2 * channels), jnp.float32),
            pltpu.SemaphoreType.DMA((2,)),
            pltpu.SemaphoreType.DMA((3,)),
            pltpu.SemaphoreType.DMA((items,)),
            pltpu.SemaphoreType.DMA((3,)),
            pltpu.SemaphoreType.REGULAR,
        ],
        compiler_params=pltpu.CompilerParams(
            collective_id=0, has_side_effects=True, vmem_limit_bytes=48 * 1024 * 1024
        ),
    )(
        queries,
        keys,
        values,
        merge_dest,
        latents,
        out_weight.T,
    )
    step_value = step_index.astype(jnp.float32)
    sigma_now = sigma_of(step_value)
    sigma_next = sigma_of(step_value + float(STRIDE))
    gain = guidance[:, None, None]
    velocity = velocities[1] + gain * (velocities[0] - velocities[1])
    denoised = latents - sigma_now[:, None, None] * velocity
    merged = slots[1] + gain * (slots[0] - slots[1])
    merged_next = slots[2] + (sigma_next - sigma_now)[:, None, None] * merged
    return denoised, merged_next


def solution(mesh):
    placed = (
        P(("jobs", "seq"), None),
        P(("jobs", "seq"), None),
        P(("jobs", "seq"), None),
        P("jobs", "seq"),
        P("jobs", "seq"),
        P("jobs", "seq", None),
        P("jobs"),
        P("jobs"),
        P(),
    )
    return jax.shard_map(
        local,
        mesh=mesh,
        in_specs=placed,
        out_specs=(P("jobs", "seq", None), P("jobs", "seq", None)),
        check_vma=False,
    )
```

```python
import functools
import math

import jax
import jax.numpy as jnp
from jax import lax
from jax.experimental import pallas as pl
from jax.experimental.pallas import tpu as pltpu
from jax.sharding import PartitionSpec as P

HEADS = 32
HD = 128
TIMESTEPS = 1000
STRIDE = 20
NEG_BIG = -1e30
SHIFT = 5.0
MESH = pl.DeviceIdType.MESH


def sigma_of(step_value):
    frac = 1.0 - step_value / TIMESTEPS
    return SHIFT * frac / (1.0 + (SHIFT - 1.0) * frac)


def sweep(first, last, body):
    if last - first <= 16:
        for index in range(first, last):
            body(index)
    else:

        def step(index, carry):
            body(index)
            return carry

        lax.fori_loop(first, last, step, 0)


def kernel(
    n,
    items,
    videos,
    query_hbm,
    key_hbm,
    value_hbm,
    dest_ref,
    latent_hbm,
    weight_hbm,
    velocity_ref,
    slot_ref,
    heads_buf,
    own,
    count_pair,
    count_buf,
    weight_twice,
    weight_rows,
    latent_buf,
    total,
    stage,
    parts,
    part_recv,
    small_sems,
    head_recv,
    send_sems,
    own_sems,
    pair_recv,
    vouched,
):
    half = n // 2
    me = lax.axis_index("seq")
    branch = me // half
    rank = me % half
    base = branch * half
    rows = query_hbm.shape[0]
    cap = rows // 2
    keys_total = half * rows
    channels = weight_hbm.shape[0]
    scale = 1.0 / math.sqrt(HD)
    sources = (query_hbm, key_hbm, value_hbm)

    barrier = pltpu.get_barrier_semaphore()

    partner = (me + half) % n

    def greet(p):
        pl.semaphore_signal(
            barrier,
            inc=1,
            device_id={"seq": base + (rank + p) % half},
            device_id_type=MESH,
        )

    sweep(1, half, greet)
    pl.semaphore_signal(barrier, inc=1, device_id={"seq": partner}, device_id_type=MESH)

    head_col = pl.multiple_of(((rank * items) % HEADS) * HD, HD)
    weight_own = weight_hbm.at[:, pl.ds(head_col, items * HD)]
    small_copies = [
        pltpu.make_async_copy(weight_own, weight_twice.at[pl.ds(0, channels)], small_sems.at[0]),
        pltpu.make_async_copy(
            weight_own, weight_twice.at[pl.ds(channels, channels)], small_sems.at[1]
        ),
        pltpu.make_async_copy(latent_hbm, latent_buf, small_sems.at[2]),
    ]
    row_at = pl.multiple_of(rank * rows, rows)

    def heads_of(which, peer, item):
        column = pl.multiple_of((peer * items + item) * HD, HD)
        return own.at[which, :, pl.ds(column, HD)]

    own_copies = [
        pltpu.make_async_copy(sources[which], own.at[which], own_sems.at[which])
        for which in range(3)
    ]
    for copy in own_copies:
        copy.start()

    count = jnp.max(dest_ref[...].astype(jnp.float32), axis=1, keepdims=True) + 1.0
    count_pair[0] = jnp.broadcast_to(count, (videos, 128)).astype(jnp.int32)
    for copy in own_copies:
        copy.wait()

    pl.semaphore_wait(barrier, half)

    partner_copy = pltpu.make_async_remote_copy(
        src_ref=count_pair.at[0],
        dst_ref=count_pair.at[1],
        send_sem=send_sems.at[0],
        recv_sem=pair_recv,
        device_id={"seq": partner},
        device_id_type=MESH,
    )
    partner_copy.start()

    def send_count(p):
        pltpu.make_async_remote_copy(
            src_ref=count_pair,
            dst_ref=count_buf.at[rank],
            send_sem=send_sems.at[3],
            recv_sem=part_recv.at[0],
            device_id={"seq": base + (rank + p) % half},
            device_id_type=MESH,
        ).start()

    for item in range(items):

        def send_heads(p):
            peer = (rank + p) % half
            for which in range(3):
                pltpu.make_async_remote_copy(
                    src_ref=heads_of(which, peer, item),
                    dst_ref=heads_buf.at[item, which, pl.ds(row_at, rows)],
                    send_sem=send_sems.at[1],
                    recv_sem=head_recv.at[item],
                    device_id={"seq": base + peer},
                    device_id_type=MESH,
                ).start()

        sweep(1, half, send_heads)

        if item == 0:
            partner_copy.wait()
            pltpu.make_async_copy(count_pair, count_buf.at[rank], part_recv.at[0]).start()
            sweep(1, half, send_count)

    for item in range(items):
        for which in range(3):
            pltpu.make_async_copy(
                heads_of(which, rank, item),
                heads_buf.at[item, which, pl.ds(row_at, rows)],
                head_recv.at[item],
            ).start()
    for copy in small_copies:
        copy.start()

    def vouch(p):
        pl.semaphore_signal(
            vouched,
            inc=1,
            device_id={"seq": base + (rank + p) % half},
            device_id_type=MESH,
        )

    sweep(1, half, vouch)

    for copy in small_copies:
        copy.wait()
    weight_rows[...] = weight_twice[...].astype(jnp.float32).T.astype(jnp.bfloat16)

    tokens = latent_buf.shape[1]
    slot_hots, latent_means, shares = [], [], []
    for v in range(videos):
        hot = lax.broadcasted_iota(jnp.int32, (cap, tokens), 0) == dest_ref[v : v + 1, :]
        hot = hot.astype(jnp.float32)
        latent_sum = jnp.dot(
            hot,
            latent_buf[v],
            precision=lax.Precision.HIGHEST,
            preferred_element_type=jnp.float32,
        )
        tally = jnp.sum(hot, axis=1, keepdims=True)
        inverse = 1.0 / jnp.maximum(tally, 1.0)
        slot_hots.append(hot)
        latent_means.append(latent_sum * inverse)
        shares.append(tally * inverse)

    pltpu.make_async_copy(count_buf, count_buf, part_recv.at[0]).wait()
    video = (rank * items) // HEADS
    lane = lax.broadcasted_iota(jnp.int32, (1, keys_total), 1)
    group_of = ((lane % rows) // cap) * half + lane // rows
    place_of = lane % cap

    def count_step(r, held):
        pair = count_buf[r]
        for side in range(2):
            row = pair[side, 0:1]
            for v in range(1, videos):
                row = jnp.where(video == v, pair[side, v : v + 1], row)
            wide = jnp.concatenate([row] * (keys_total // 128), axis=1)
            owner = (side * half + base) % n + r
            held = jnp.where(group_of == owner, wide, held)
        return held

    held = jnp.zeros((1, keys_total), jnp.int32)
    if half <= 16:
        for r in range(half):
            held = count_step(r, held)
    else:
        held = lax.fori_loop(0, half, count_step, held)
    live = place_of < held

    def by_blocks(block, body):
        if keys_total <= 4 * block:
            for index in range(keys_total // block):
                body(index)
        else:

            def step(index, carry):
                body(index)
                return carry

            lax.fori_loop(0, keys_total // block, step, 0)

    left = lax.broadcasted_iota(jnp.int32, (cap // 2, 2 * channels), 1) < channels

    for item in range(items):
        pltpu.make_async_copy(heads_buf.at[item], heads_buf.at[item], head_recv.at[item]).wait()

        block = min(keys_total, 256)

        def attend(index):
            at = pl.ds(pl.multiple_of(index * block, block), block)
            scores = (
                lax.dot_general(
                    heads_buf[item, 0, at, :],
                    heads_buf[item, 1],
                    (((1,), (1,)), ((), ())),
                    preferred_element_type=jnp.float32,
                )
                * scale
            )
            scores = jnp.where(live, scores, NEG_BIG)
            weights = jnp.exp(scores - jnp.max(scores, axis=-1, keepdims=True))
            inverse = 1.0 / jnp.sum(weights, axis=-1, keepdims=True)
            probs = (weights * inverse).astype(jnp.bfloat16)
            attended = jnp.dot(
                probs, heads_buf[item, 2], preferred_element_type=jnp.float32
            ).astype(jnp.bfloat16)
            term = jnp.dot(
                attended,
                weight_rows[item * HD : (item + 1) * HD, :],
                preferred_element_type=jnp.float32,
            )
            if item == 0:
                total[at, :] = term
            else:
                total[at, :] += term

        by_blocks(block, attend)

    both = total[...].reshape(half, 2, 2, cap // 2, 2 * channels)
    stage[...] = jnp.where(left, both[:, :, 0], both[:, :, 1])

    pl.semaphore_wait(vouched, half - 1)

    def send_part(p):
        owner = (me + p) % n
        pltpu.make_async_remote_copy(
            src_ref=stage.at[owner % half, owner // half],
            dst_ref=parts.at[me],
            send_sem=send_sems.at[2],
            recv_sem=part_recv.at[1],
            device_id={"seq": owner},
            device_id_type=MESH,
        ).start()

    sweep(1, n, send_part)
    pltpu.make_async_copy(stage.at[rank, branch], parts.at[me], part_recv.at[1]).start()
    pltpu.make_async_copy(parts, parts, part_recv.at[1]).wait()

    span = half // videos
    for v in range(videos):
        cond = jnp.sum(parts[v * span : (v + 1) * span], axis=0)
        uncond = jnp.sum(parts[half + v * span : half + (v + 1) * span], axis=0)
        merged = jnp.concatenate(
            [
                jnp.where(left, cond, pltpu.roll(uncond, channels, 1)),
                jnp.where(left, pltpu.roll(cond, channels, 1), uncond),
            ],
            axis=0,
        )
        velocity = lax.dot_general(
            slot_hots[v],
            merged,
            (((0,), (0,)), ((), ())),
            precision=lax.Precision.HIGHEST,
            preferred_element_type=jnp.float32,
        )
        velocity_ref[0, v] = velocity[:, :channels]
        velocity_ref[1, v] = velocity[:, channels:]
        merged = shares[v] * merged
        slot_ref[0, v] = merged[:, :channels]
        slot_ref[1, v] = merged[:, channels:]
        slot_ref[2, v] = latent_means[v]

    pltpu.make_async_copy(
        count_buf.at[pl.ds(0, half - 1)], count_buf.at[pl.ds(0, half - 1)], send_sems.at[3]
    ).wait()
    sent = heads_buf.at[:, :, pl.ds(0, (half - 1) * rows)]
    pltpu.make_async_copy(sent, sent, send_sems.at[1]).wait()
    pltpu.make_async_copy(
        parts.at[pl.ds(0, n - 1)], parts.at[pl.ds(0, n - 1)], send_sems.at[2]
    ).wait()


def local(
    queries, keys, values, live_counts, merge_dest, latents, guidance, step_index, out_weight
):
    n = lax.axis_size("seq")
    half = n // 2
    rows, columns = queries.shape
    videos, tokens, channels = latents.shape
    items = columns // HD // half
    cap = rows // 2
    outside = pl.BlockSpec(memory_space=pltpu.HBM)
    inside = pl.BlockSpec(memory_space=pltpu.VMEM)
    velocities, slots = pl.pallas_call(
        functools.partial(kernel, n, items, videos),
        out_shape=(
            jax.ShapeDtypeStruct((2, videos, tokens, channels), jnp.float32),
            jax.ShapeDtypeStruct((3, videos, cap, channels), jnp.float32),
        ),
        in_specs=[outside] * 3 + [inside] + [outside] * 2,
        out_specs=(inside, inside),
        scratch_shapes=[
            pltpu.VMEM((items, 3, half * rows, HD), jnp.bfloat16),
            pltpu.VMEM((3, rows, columns), jnp.bfloat16),
            pltpu.VMEM((2, videos, 128), jnp.int32),
            pltpu.VMEM((half, 2, videos, 128), jnp.int32),
            pltpu.VMEM((2 * channels, items * HD), jnp.bfloat16),
            pltpu.VMEM((items * HD, 2 * channels), jnp.bfloat16),
            pltpu.VMEM((videos, tokens, channels), jnp.float32),
            pltpu.VMEM((half * rows, 2 * channels), jnp.float32),
            pltpu.VMEM((half, 2, cap // 2, 2 * channels), jnp.float32),
            pltpu.VMEM((n, cap // 2, 2 * channels), jnp.float32),
            pltpu.SemaphoreType.DMA((2,)),
            pltpu.SemaphoreType.DMA((3,)),
            pltpu.SemaphoreType.DMA((items,)),
            pltpu.SemaphoreType.DMA((4,)),
            pltpu.SemaphoreType.DMA((3,)),
            pltpu.SemaphoreType.DMA,
            pltpu.SemaphoreType.REGULAR,
        ],
        compiler_params=pltpu.CompilerParams(
            collective_id=0, has_side_effects=True, vmem_limit_bytes=55040 * 1024
        ),
    )(
        queries,
        keys,
        values,
        merge_dest,
        latents,
        out_weight.T,
    )
    step_value = step_index.astype(jnp.float32)
    sigma_now = sigma_of(step_value)
    sigma_next = sigma_of(step_value + float(STRIDE))
    gain = guidance[:, None, None]
    velocity = velocities[1] + gain * (velocities[0] - velocities[1])
    denoised = latents - sigma_now[:, None, None] * velocity
    merged = slots[1] + gain * (slots[0] - slots[1])
    merged_next = slots[2] + (sigma_next - sigma_now)[:, None, None] * merged
    return denoised, merged_next


def solution(mesh):
    placed = (
        P(("jobs", "seq"), None),
        P(("jobs", "seq"), None),
        P(("jobs", "seq"), None),
        P("jobs", "seq"),
        P("jobs", "seq"),
        P("jobs", "seq", None),
        P("jobs"),
        P("jobs"),
        P(),
    )
    return jax.shard_map(
        local,
        mesh=mesh,
        in_specs=placed,
        out_specs=(P("jobs", "seq", None), P("jobs", "seq", None)),
        check_vma=False,
    )
```

```python
import functools
import math

import jax
import jax.numpy as jnp
from jax import lax
from jax.experimental import pallas as pl
from jax.experimental.pallas import tpu as pltpu
from jax.sharding import PartitionSpec as P

HEADS = 32
HD = 128
TIMESTEPS = 1000
STRIDE = 20
NEG_BIG = -1e30
SHIFT = 5.0
MESH = pl.DeviceIdType.MESH


def sigma_of(step_value):
    frac = 1.0 - step_value / TIMESTEPS
    return SHIFT * frac / (1.0 + (SHIFT - 1.0) * frac)


def sweep(first, last, body, longest=16):
    if last - first <= longest:
        for index in range(first, last):
            body(index)
    else:

        def step(index, carry):
            body(index)
            return carry

        lax.fori_loop(first, last, step, 0)


def kernel(
    n,
    items,
    videos,
    query_hbm,
    key_hbm,
    value_hbm,
    dest_ref,
    latent_hbm,
    weight_hbm,
    velocity_ref,
    slot_ref,
    heads_buf,
    own,
    laid,
    count_pair,
    count_buf,
    weight_twice,
    weight_rows,
    latent_buf,
    total,
    stage,
    parts,
    part_recv,
    small_sems,
    head_recv,
    send_sems,
    own_sems,
    pair_recv,
    vouched,
):
    half = n // 2
    me = lax.axis_index("seq")
    branch = me // half
    rank = me % half
    base = branch * half
    rows, columns = query_hbm.shape
    cap = rows // 2
    keys_total = half * rows
    channels = weight_hbm.shape[0]
    scale = 1.0 / math.sqrt(HD)
    sources = (query_hbm, key_hbm, value_hbm)

    barrier = pltpu.get_barrier_semaphore()

    partner = (me + half) % n

    def greet(p):
        pl.semaphore_signal(
            barrier,
            inc=1,
            device_id={"seq": base + (rank + p) % half},
            device_id_type=MESH,
        )

    sweep(1, half, greet)
    pl.semaphore_signal(barrier, inc=1, device_id={"seq": partner}, device_id_type=MESH)

    head_col = pl.multiple_of(((rank * items) % HEADS) * HD, HD)
    weight_own = weight_hbm.at[:, pl.ds(head_col, items * HD)]
    small_copies = [
        pltpu.make_async_copy(weight_own, weight_twice.at[pl.ds(0, channels)], small_sems.at[0]),
        pltpu.make_async_copy(
            weight_own, weight_twice.at[pl.ds(channels, channels)], small_sems.at[1]
        ),
        pltpu.make_async_copy(latent_hbm, latent_buf, small_sems.at[2]),
    ]

    own_copies = [
        pltpu.make_async_copy(sources[which], own.at[which], own_sems.at[which])
        for which in range(3)
    ]
    for copy in own_copies:
        copy.start()

    count = jnp.max(dest_ref[...].astype(jnp.float32), axis=1, keepdims=True) + 1.0
    count_pair[0] = jnp.broadcast_to(count, (videos, 128)).astype(jnp.int32)
    for copy in own_copies:
        copy.wait()

    def lay(head):
        for which in range(3):
            column = head * HD if isinstance(head, int) else pl.multiple_of(head * HD, HD)
            laid[head, which] = own[which, :, pl.ds(column, HD)]

    sweep(0, columns // HD, lay, 32)

    pl.semaphore_wait(barrier, half)

    partner_copy = pltpu.make_async_remote_copy(
        src_ref=count_pair.at[0],
        dst_ref=count_pair.at[1],
        send_sem=send_sems.at[0],
        recv_sem=pair_recv,
        device_id={"seq": partner},
        device_id_type=MESH,
    )
    partner_copy.start()

    def send_count(p):
        pltpu.make_async_remote_copy(
            src_ref=count_pair,
            dst_ref=count_buf.at[rank],
            send_sem=send_sems.at[3],
            recv_sem=part_recv.at[0],
            device_id={"seq": base + (rank + p) % half},
            device_id_type=MESH,
        ).start()

    for item in range(items):

        def send_heads(p):
            peer = (rank + p) % half
            pltpu.make_async_remote_copy(
                src_ref=laid.at[peer * items + item],
                dst_ref=heads_buf.at[item, rank],
                send_sem=send_sems.at[1],
                recv_sem=head_recv.at[item],
                device_id={"seq": base + peer},
                device_id_type=MESH,
            ).start()

        sweep(1, half, send_heads)

        if item == 0:
            partner_copy.wait()
            pltpu.make_async_copy(count_pair, count_buf.at[rank], part_recv.at[0]).start()
            sweep(1, half, send_count)

    for item in range(items):
        pltpu.make_async_copy(
            laid.at[rank * items + item], heads_buf.at[item, rank], head_recv.at[item]
        ).start()
    for copy in small_copies:
        copy.start()

    def vouch(p):
        pl.semaphore_signal(
            vouched,
            inc=1,
            device_id={"seq": base + (rank + p) % half},
            device_id_type=MESH,
        )

    sweep(1, half, vouch)

    for copy in small_copies:
        copy.wait()
    weight_rows[...] = weight_twice[...].astype(jnp.float32).T.astype(jnp.bfloat16)

    tokens = latent_buf.shape[1]
    slot_hots, latent_means, shares = [], [], []
    for v in range(videos):
        hot = lax.broadcasted_iota(jnp.int32, (cap, tokens), 0) == dest_ref[v : v + 1, :]
        hot = hot.astype(jnp.float32)
        latent_sum = jnp.dot(
            hot,
            latent_buf[v],
            precision=lax.Precision.HIGHEST,
            preferred_element_type=jnp.float32,
        )
        tally = jnp.sum(hot, axis=1, keepdims=True)
        inverse = 1.0 / jnp.maximum(tally, 1.0)
        slot_hots.append(jnp.concatenate([hot.T] * 3, axis=1).astype(jnp.bfloat16))
        latent_means.append(latent_sum * inverse)
        shares.append(tally * inverse)

    pltpu.make_async_copy(count_buf, count_buf, part_recv.at[0]).wait()
    video = (rank * items) // HEADS
    lane = lax.broadcasted_iota(jnp.int32, (1, keys_total), 1)
    group_of = ((lane % rows) // cap) * half + lane // rows
    place_of = lane % cap

    def count_step(r, held):
        pair = count_buf[r]
        for side in range(2):
            row = pair[side, 0:1]
            for v in range(1, videos):
                row = jnp.where(video == v, pair[side, v : v + 1], row)
            wide = jnp.concatenate([row] * (keys_total // 128), axis=1)
            owner = (side * half + base) % n + r
            held = jnp.where(group_of == owner, wide, held)
        return held

    held = jnp.zeros((1, keys_total), jnp.int32)
    if half <= 16:
        for r in range(half):
            held = count_step(r, held)
    else:
        held = lax.fori_loop(0, half, count_step, held)
    live = place_of < held

    def by_blocks(block, body):
        if keys_total <= 4 * block:
            for index in range(keys_total // block):
                body(index)
        else:

            def step(index, carry):
                body(index)
                return carry

            lax.fori_loop(0, keys_total // block, step, 0)

    left = lax.broadcasted_iota(jnp.int32, (cap // 2, 2 * channels), 1) < channels

    for item in range(items):
        pltpu.make_async_copy(heads_buf.at[item], heads_buf.at[item], head_recv.at[item]).wait()

        block = min(keys_total, 256)

        key_rows = heads_buf[item, :, 1].reshape(keys_total, HD)
        value_rows = heads_buf[item, :, 2].reshape(keys_total, HD)
        ranks = block // rows

        def attend(index):
            at = pl.ds(pl.multiple_of(index * block, block), block)
            query_rows = heads_buf[item, pl.ds(index * ranks, ranks), 0].reshape(block, HD)
            scores = (
                lax.dot_general(
                    query_rows,
                    key_rows,
                    (((1,), (1,)), ((), ())),
                    preferred_element_type=jnp.float32,
                )
                * scale
            )
            scores = jnp.where(live, scores, NEG_BIG)
            weights = jnp.exp(scores - jnp.max(scores, axis=-1, keepdims=True))
            inverse = 1.0 / jnp.sum(weights, axis=-1, keepdims=True)
            probs = (weights * inverse).astype(jnp.bfloat16)
            attended = jnp.dot(
                probs, value_rows, preferred_element_type=jnp.float32
            ).astype(jnp.bfloat16)
            term = jnp.dot(
                attended,
                weight_rows[item * HD : (item + 1) * HD, :],
                preferred_element_type=jnp.float32,
            )
            if item == 0:
                total[at, :] = term
            else:
                total[at, :] += term

        by_blocks(block, attend)

    both = total[...].reshape(half, 2, 2, cap // 2, 2 * channels)
    stage[...] = jnp.where(left, both[:, :, 0], both[:, :, 1])

    pl.semaphore_wait(vouched, half - 1)

    def send_part(side, peer):
        pltpu.make_async_remote_copy(
            src_ref=stage.at[peer, side],
            dst_ref=parts.at[me],
            send_sem=send_sems.at[2],
            recv_sem=part_recv.at[1],
            device_id={"seq": side * half + peer},
            device_id_type=MESH,
        ).start()

    sweep(0, half, lambda p: send_part(1 - branch, (rank + p) % half))
    sweep(1, half, lambda p: send_part(branch, (rank + p) % half))
    pltpu.make_async_copy(stage.at[rank, branch], parts.at[me], part_recv.at[1]).start()
    pltpu.make_async_copy(parts, parts, part_recv.at[1]).wait()

    span = half // videos
    for v in range(videos):
        cond = jnp.sum(parts[v * span : (v + 1) * span], axis=0)
        uncond = jnp.sum(parts[half + v * span : half + (v + 1) * span], axis=0)
        merged = jnp.concatenate(
            [
                jnp.where(left, cond, pltpu.roll(uncond, channels, 1)),
                jnp.where(left, pltpu.roll(cond, channels, 1), uncond),
            ],
            axis=0,
        )
        terms, rest = [], merged
        for _ in range(3):
            terms.append(rest.astype(jnp.bfloat16))
            rest = rest - terms[-1].astype(jnp.float32)
        velocity = jnp.dot(
            slot_hots[v],
            jnp.concatenate(terms, axis=0),
            preferred_element_type=jnp.float32,
        )
        velocity_ref[0, v] = velocity[:, :channels]
        velocity_ref[1, v] = velocity[:, channels:]
        merged = shares[v] * merged
        slot_ref[0, v] = merged[:, :channels]
        slot_ref[1, v] = merged[:, channels:]
        slot_ref[2, v] = latent_means[v]

    pltpu.make_async_copy(
        count_buf.at[pl.ds(0, half - 1)], count_buf.at[pl.ds(0, half - 1)], send_sems.at[3]
    ).wait()
    sent = heads_buf.at[:, pl.ds(0, half - 1)]
    pltpu.make_async_copy(sent, sent, send_sems.at[1]).wait()
    pltpu.make_async_copy(
        parts.at[pl.ds(0, n - 1)], parts.at[pl.ds(0, n - 1)], send_sems.at[2]
    ).wait()


def local(
    queries, keys, values, live_counts, merge_dest, latents, guidance, step_index, out_weight
):
    n = lax.axis_size("seq")
    half = n // 2
    rows, columns = queries.shape
    videos, tokens, channels = latents.shape
    items = columns // HD // half
    cap = rows // 2
    outside = pl.BlockSpec(memory_space=pltpu.HBM)
    inside = pl.BlockSpec(memory_space=pltpu.VMEM)
    velocities, slots = pl.pallas_call(
        functools.partial(kernel, n, items, videos),
        out_shape=(
            jax.ShapeDtypeStruct((2, videos, tokens, channels), jnp.float32),
            jax.ShapeDtypeStruct((3, videos, cap, channels), jnp.float32),
        ),
        in_specs=[outside] * 3 + [inside] + [outside] * 2,
        out_specs=(inside, inside),
        scratch_shapes=[
            pltpu.VMEM((items, half, 3, rows, HD), jnp.bfloat16),
            pltpu.VMEM((3, rows, columns), jnp.bfloat16),
            pltpu.VMEM((columns // HD, 3, rows, HD), jnp.bfloat16),
            pltpu.VMEM((2, videos, 128), jnp.int32),
            pltpu.VMEM((half, 2, videos, 128), jnp.int32),
            pltpu.VMEM((2 * channels, items * HD), jnp.bfloat16),
            pltpu.VMEM((items * HD, 2 * channels), jnp.bfloat16),
            pltpu.VMEM((videos, tokens, channels), jnp.float32),
            pltpu.VMEM((half * rows, 2 * channels), jnp.float32),
            pltpu.VMEM((half, 2, cap // 2, 2 * channels), jnp.float32),
            pltpu.VMEM((n, cap // 2, 2 * channels), jnp.float32),
            pltpu.SemaphoreType.DMA((2,)),
            pltpu.SemaphoreType.DMA((3,)),
            pltpu.SemaphoreType.DMA((items,)),
            pltpu.SemaphoreType.DMA((4,)),
            pltpu.SemaphoreType.DMA((3,)),
            pltpu.SemaphoreType.DMA,
            pltpu.SemaphoreType.REGULAR,
        ],
        compiler_params=pltpu.CompilerParams(
            collective_id=0, has_side_effects=True, vmem_limit_bytes=55040 * 1024
        ),
    )(
        queries,
        keys,
        values,
        merge_dest,
        latents,
        out_weight.T,
    )
    step_value = step_index.astype(jnp.float32)
    sigma_now = sigma_of(step_value)
    sigma_next = sigma_of(step_value + float(STRIDE))
    gain = guidance[:, None, None]
    velocity = velocities[1] + gain * (velocities[0] - velocities[1])
    denoised = latents - sigma_now[:, None, None] * velocity
    merged = slots[1] + gain * (slots[0] - slots[1])
    merged_next = slots[2] + (sigma_next - sigma_now)[:, None, None] * merged
    return denoised, merged_next


def solution(mesh):
    placed = (
        P(("jobs", "seq"), None),
        P(("jobs", "seq"), None),
        P(("jobs", "seq"), None),
        P("jobs", "seq"),
        P("jobs", "seq"),
        P("jobs", "seq", None),
        P("jobs"),
        P("jobs"),
        P(),
    )
    return jax.shard_map(
        local,
        mesh=mesh,
        in_specs=placed,
        out_specs=(P("jobs", "seq", None), P("jobs", "seq", None)),
        check_vma=False,
    )
```

```python
import functools
import math

import jax
import jax.numpy as jnp
from jax import lax
from jax.experimental import pallas as pl
from jax.experimental.pallas import tpu as pltpu
from jax.sharding import PartitionSpec as P

HEADS = 32
HD = 128
TIMESTEPS = 1000
STRIDE = 20
NEG_BIG = -1e30
SHIFT = 5.0
MESH = pl.DeviceIdType.MESH


def sigma_of(step_value):
    frac = 1.0 - step_value / TIMESTEPS
    return SHIFT * frac / (1.0 + (SHIFT - 1.0) * frac)


def sweep(first, last, body, longest=16):
    if last - first <= longest:
        for index in range(first, last):
            body(index)
    else:

        def step(index, carry):
            body(index)
            return carry

        lax.fori_loop(first, last, step, 0)


def kernel(
    n,
    items,
    videos,
    query_hbm,
    key_hbm,
    value_hbm,
    dest_ref,
    latent_hbm,
    weight_hbm,
    velocity_ref,
    slot_ref,
    heads_buf,
    own,
    laid,
    count_pair,
    count_buf,
    weight_twice,
    weight_rows,
    latent_buf,
    total,
    stage,
    parts,
    part_recv,
    small_sems,
    head_recv,
    send_sems,
    own_sems,
    pair_recv,
    vouched,
):
    half = n // 2
    me = lax.axis_index("seq")
    branch = me // half
    rank = me % half
    base = branch * half
    rows, columns = query_hbm.shape
    cap = rows // 2
    keys_total = half * rows
    channels = weight_hbm.shape[0]
    scale = 1.0 / math.sqrt(HD)
    sources = (query_hbm, key_hbm, value_hbm)

    barrier = pltpu.get_barrier_semaphore()

    partner = (me + half) % n

    def greet(p):
        pl.semaphore_signal(
            barrier,
            inc=1,
            device_id={"seq": base + (rank + p) % half},
            device_id_type=MESH,
        )

    sweep(1, half, greet)
    pl.semaphore_signal(barrier, inc=1, device_id={"seq": partner}, device_id_type=MESH)

    head_col = pl.multiple_of(((rank * items) % HEADS) * HD, HD)
    weight_own = weight_hbm.at[:, pl.ds(head_col, items * HD)]
    small_copies = [
        pltpu.make_async_copy(weight_own, weight_twice.at[pl.ds(0, channels)], small_sems.at[0]),
        pltpu.make_async_copy(
            weight_own, weight_twice.at[pl.ds(channels, channels)], small_sems.at[1]
        ),
        pltpu.make_async_copy(latent_hbm, latent_buf, small_sems.at[2]),
    ]

    own_copies = [
        pltpu.make_async_copy(sources[which], own.at[which], own_sems.at[which])
        for which in range(3)
    ]
    for copy in own_copies:
        copy.start()

    count = jnp.max(dest_ref[...].astype(jnp.float32), axis=1, keepdims=True) + 1.0
    count_pair[0] = jnp.broadcast_to(count, (videos, 128)).astype(jnp.int32)
    for copy in own_copies:
        copy.wait()

    def lay(head):
        for which in range(3):
            column = head * HD if isinstance(head, int) else pl.multiple_of(head * HD, HD)
            laid[head, which] = own[which, :, pl.ds(column, HD)]

    sweep(0, columns // HD, lay, 32)

    pl.semaphore_wait(barrier, half)

    partner_copy = pltpu.make_async_remote_copy(
        src_ref=count_pair.at[0],
        dst_ref=count_pair.at[1],
        send_sem=send_sems.at[0],
        recv_sem=pair_recv,
        device_id={"seq": partner},
        device_id_type=MESH,
    )
    partner_copy.start()

    def send_count(p):
        pltpu.make_async_remote_copy(
            src_ref=count_pair,
            dst_ref=count_buf.at[rank],
            send_sem=send_sems.at[3],
            recv_sem=part_recv.at[0],
            device_id={"seq": base + (rank + p) % half},
            device_id_type=MESH,
        ).start()

    bits = (half - 1).bit_length()
    core = rank % 2

    def peer_at(p):
        if half != 1 << bits or half < 4:
            return (rank + p) % half
        away, other = p // 2, p % 2
        turned = sum(((away // 2**k) % 2) * 2 ** (bits - 2 - k) for k in range(bits - 1))
        step = 2 * (away * (1 - core) + turned * core) + other
        return sum(((rank // 2**k + step // 2**k) % 2) * 2**k for k in range(bits))

    for item in range(items):

        def send_heads(p):
            peer = peer_at(p)
            pltpu.make_async_remote_copy(
                src_ref=laid.at[peer * items + item],
                dst_ref=heads_buf.at[item, rank],
                send_sem=send_sems.at[1],
                recv_sem=head_recv.at[item],
                device_id={"seq": base + peer},
                device_id_type=MESH,
            ).start()

        sweep(2, half, send_heads)
        send_heads(1)

        if item == 0:
            partner_copy.wait()
            pltpu.make_async_copy(count_pair, count_buf.at[rank], part_recv.at[0]).start()
            sweep(1, half, send_count)

    for item in range(items):
        pltpu.make_async_copy(
            laid.at[rank * items + item], heads_buf.at[item, rank], head_recv.at[item]
        ).start()
    for copy in small_copies:
        copy.start()

    def vouch(p):
        pl.semaphore_signal(
            vouched,
            inc=1,
            device_id={"seq": base + (rank + p) % half},
            device_id_type=MESH,
        )

    sweep(1, half, vouch)

    for copy in small_copies:
        copy.wait()
    weight_rows[...] = weight_twice[...].astype(jnp.float32).T.astype(jnp.bfloat16)

    tokens = latent_buf.shape[1]
    slot_hots, latent_means, shares = [], [], []
    for v in range(videos):
        hot = lax.broadcasted_iota(jnp.int32, (cap, tokens), 0) == dest_ref[v : v + 1, :]
        hot = hot.astype(jnp.float32)
        latent_sum = jnp.dot(
            hot,
            latent_buf[v],
            precision=lax.Precision.HIGHEST,
            preferred_element_type=jnp.float32,
        )
        tally = jnp.sum(hot, axis=1, keepdims=True)
        inverse = 1.0 / jnp.maximum(tally, 1.0)
        slot_hots.append(jnp.concatenate([hot.T] * 3, axis=1).astype(jnp.bfloat16))
        latent_means.append(latent_sum * inverse)
        shares.append(tally * inverse)

    pltpu.make_async_copy(count_buf, count_buf, part_recv.at[0]).wait()
    video = (rank * items) // HEADS
    lane = lax.broadcasted_iota(jnp.int32, (1, keys_total), 1)
    group_of = ((lane % rows) // cap) * half + lane // rows
    place_of = lane % cap

    def count_step(r, held):
        pair = count_buf[r]
        for side in range(2):
            row = pair[side, 0:1]
            for v in range(1, videos):
                row = jnp.where(video == v, pair[side, v : v + 1], row)
            wide = jnp.concatenate([row] * (keys_total // 128), axis=1)
            owner = (side * half + base) % n + r
            held = jnp.where(group_of == owner, wide, held)
        return held

    held = jnp.zeros((1, keys_total), jnp.int32)
    if half <= 16:
        for r in range(half):
            held = count_step(r, held)
    else:
        held = lax.fori_loop(0, half, count_step, held)
    live = place_of < held

    def by_blocks(block, body):
        if keys_total <= 4 * block:
            for index in range(keys_total // block):
                body(index)
        else:

            def step(index, carry):
                body(index)
                return carry

            lax.fori_loop(0, keys_total // block, step, 0)

    left = lax.broadcasted_iota(jnp.int32, (cap // 2, 2 * channels), 1) < channels

    for item in range(items):
        pltpu.make_async_copy(heads_buf.at[item], heads_buf.at[item], head_recv.at[item]).wait()

        block = min(keys_total, 256)

        key_rows = heads_buf[item, :, 1].reshape(keys_total, HD)
        value_rows = heads_buf[item, :, 2].reshape(keys_total, HD)
        ranks = block // rows

        def attend(index):
            at = pl.ds(pl.multiple_of(index * block, block), block)
            query_rows = heads_buf[item, pl.ds(index * ranks, ranks), 0].reshape(block, HD)
            scores = (
                lax.dot_general(
                    query_rows,
                    key_rows,
                    (((1,), (1,)), ((), ())),
                    preferred_element_type=jnp.float32,
                )
                * scale
            )
            scores = jnp.where(live, scores, NEG_BIG)
            weights = jnp.exp(scores - jnp.max(scores, axis=-1, keepdims=True))
            inverse = 1.0 / jnp.sum(weights, axis=-1, keepdims=True)
            probs = (weights * inverse).astype(jnp.bfloat16)
            attended = jnp.dot(
                probs, value_rows, preferred_element_type=jnp.float32
            ).astype(jnp.bfloat16)
            term = jnp.dot(
                attended,
                weight_rows[item * HD : (item + 1) * HD, :],
                preferred_element_type=jnp.float32,
            )
            if item == 0:
                total[at, :] = term
            else:
                total[at, :] += term

        by_blocks(block, attend)

    both = total[...].reshape(half, 2, 2, cap // 2, 2 * channels)
    stage[...] = jnp.where(left, both[:, :, 0], both[:, :, 1])

    pl.semaphore_wait(vouched, half - 1)

    def send_part(side, peer):
        pltpu.make_async_remote_copy(
            src_ref=stage.at[peer, side],
            dst_ref=parts.at[me],
            send_sem=send_sems.at[2],
            recv_sem=part_recv.at[1],
            device_id={"seq": side * half + peer},
            device_id_type=MESH,
        ).start()

    sweep(0, half, lambda p: send_part(1 - branch, (rank + p) % half))
    sweep(1, half, lambda p: send_part(branch, (rank + p) % half))
    pltpu.make_async_copy(stage.at[rank, branch], parts.at[me], part_recv.at[1]).start()
    pltpu.make_async_copy(parts, parts, part_recv.at[1]).wait()

    span = half // videos
    for v in range(videos):
        cond = jnp.sum(parts[v * span : (v + 1) * span], axis=0)
        uncond = jnp.sum(parts[half + v * span : half + (v + 1) * span], axis=0)
        merged = jnp.concatenate(
            [
                jnp.where(left, cond, pltpu.roll(uncond, channels, 1)),
                jnp.where(left, pltpu.roll(cond, channels, 1), uncond),
            ],
            axis=0,
        )
        terms, rest = [], merged
        for _ in range(3):
            terms.append(rest.astype(jnp.bfloat16))
            rest = rest - terms[-1].astype(jnp.float32)
        velocity = jnp.dot(
            slot_hots[v],
            jnp.concatenate(terms, axis=0),
            preferred_element_type=jnp.float32,
        )
        velocity_ref[0, v] = velocity[:, :channels]
        velocity_ref[1, v] = velocity[:, channels:]
        merged = shares[v] * merged
        slot_ref[0, v] = merged[:, :channels]
        slot_ref[1, v] = merged[:, channels:]
        slot_ref[2, v] = latent_means[v]

    pltpu.make_async_copy(
        count_buf.at[pl.ds(0, half - 1)], count_buf.at[pl.ds(0, half - 1)], send_sems.at[3]
    ).wait()
    sent = heads_buf.at[:, pl.ds(0, half - 1)]
    pltpu.make_async_copy(sent, sent, send_sems.at[1]).wait()
    pltpu.make_async_copy(
        parts.at[pl.ds(0, n - 1)], parts.at[pl.ds(0, n - 1)], send_sems.at[2]
    ).wait()


def local(
    queries, keys, values, live_counts, merge_dest, latents, guidance, step_index, out_weight
):
    n = lax.axis_size("seq")
    half = n // 2
    rows, columns = queries.shape
    videos, tokens, channels = latents.shape
    items = columns // HD // half
    cap = rows // 2
    outside = pl.BlockSpec(memory_space=pltpu.HBM)
    inside = pl.BlockSpec(memory_space=pltpu.VMEM)
    velocities, slots = pl.pallas_call(
        functools.partial(kernel, n, items, videos),
        out_shape=(
            jax.ShapeDtypeStruct((2, videos, tokens, channels), jnp.float32),
            jax.ShapeDtypeStruct((3, videos, cap, channels), jnp.float32),
        ),
        in_specs=[outside] * 3 + [inside] + [outside] * 2,
        out_specs=(inside, inside),
        scratch_shapes=[
            pltpu.VMEM((items, half, 3, rows, HD), jnp.bfloat16),
            pltpu.VMEM((3, rows, columns), jnp.bfloat16),
            pltpu.VMEM((columns // HD, 3, rows, HD), jnp.bfloat16),
            pltpu.VMEM((2, videos, 128), jnp.int32),
            pltpu.VMEM((half, 2, videos, 128), jnp.int32),
            pltpu.VMEM((2 * channels, items * HD), jnp.bfloat16),
            pltpu.VMEM((items * HD, 2 * channels), jnp.bfloat16),
            pltpu.VMEM((videos, tokens, channels), jnp.float32),
            pltpu.VMEM((half * rows, 2 * channels), jnp.float32),
            pltpu.VMEM((half, 2, cap // 2, 2 * channels), jnp.float32),
            pltpu.VMEM((n, cap // 2, 2 * channels), jnp.float32),
            pltpu.SemaphoreType.DMA((2,)),
            pltpu.SemaphoreType.DMA((3,)),
            pltpu.SemaphoreType.DMA((items,)),
            pltpu.SemaphoreType.DMA((4,)),
            pltpu.SemaphoreType.DMA((3,)),
            pltpu.SemaphoreType.DMA,
            pltpu.SemaphoreType.REGULAR,
        ],
        compiler_params=pltpu.CompilerParams(
            collective_id=0, has_side_effects=True, vmem_limit_bytes=55040 * 1024
        ),
    )(
        queries,
        keys,
        values,
        merge_dest,
        latents,
        out_weight.T,
    )
    step_value = step_index.astype(jnp.float32)
    sigma_now = sigma_of(step_value)
    sigma_next = sigma_of(step_value + float(STRIDE))
    gain = guidance[:, None, None]
    velocity = velocities[1] + gain * (velocities[0] - velocities[1])
    denoised = latents - sigma_now[:, None, None] * velocity
    merged = slots[1] + gain * (slots[0] - slots[1])
    merged_next = slots[2] + (sigma_next - sigma_now)[:, None, None] * merged
    return denoised, merged_next


def solution(mesh):
    placed = (
        P(("jobs", "seq"), None),
        P(("jobs", "seq"), None),
        P(("jobs", "seq"), None),
        P("jobs", "seq"),
        P("jobs", "seq"),
        P("jobs", "seq", None),
        P("jobs"),
        P("jobs"),
        P(),
    )
    return jax.shard_map(
        local,
        mesh=mesh,
        in_specs=placed,
        out_specs=(P("jobs", "seq", None), P("jobs", "seq", None)),
        check_vma=False,
    )
```

```python
import functools
import math

import jax
import jax.numpy as jnp
from jax import lax
from jax.experimental import pallas as pl
from jax.experimental.pallas import tpu as pltpu
from jax.sharding import PartitionSpec as P

HEADS = 32
HD = 128
TIMESTEPS = 1000
STRIDE = 20
NEG_BIG = -1e30
SHIFT = 5.0
MESH = pl.DeviceIdType.MESH


def sigma_of(step_value):
    frac = 1.0 - step_value / TIMESTEPS
    return SHIFT * frac / (1.0 + (SHIFT - 1.0) * frac)


def sweep(first, last, body, longest=16):
    if last - first <= longest:
        for index in range(first, last):
            body(index)
    else:

        def step(index, carry):
            body(index)
            return carry

        lax.fori_loop(first, last, step, 0)


def kernel(
    n,
    items,
    videos,
    query_hbm,
    key_hbm,
    value_hbm,
    dest_ref,
    latent_hbm,
    weight_hbm,
    velocity_ref,
    slot_ref,
    heads_buf,
    own,
    laid,
    count_pair,
    count_buf,
    weight_twice,
    weight_rows,
    latent_buf,
    total,
    stage,
    parts,
    part_recv,
    small_sems,
    head_recv,
    send_sems,
    own_sems,
    pair_recv,
    vouched,
):
    half = n // 2
    me = lax.axis_index("seq")
    branch = me // half
    rank = me % half
    base = branch * half
    rows, columns = query_hbm.shape
    cap = rows // 2
    keys_total = half * rows
    channels = weight_hbm.shape[0]
    scale = 1.0 / math.sqrt(HD)
    sources = (query_hbm, key_hbm, value_hbm)

    barrier = pltpu.get_barrier_semaphore()

    partner = (me + half) % n

    def greet(p):
        pl.semaphore_signal(
            barrier,
            inc=1,
            device_id={"seq": base + (rank + p) % half},
            device_id_type=MESH,
        )

    sweep(1, half, greet)
    pl.semaphore_signal(barrier, inc=1, device_id={"seq": partner}, device_id_type=MESH)

    head_col = pl.multiple_of(((rank * items) % HEADS) * HD, HD)
    weight_own = weight_hbm.at[:, pl.ds(head_col, items * HD)]
    small_copies = [
        pltpu.make_async_copy(weight_own, weight_twice.at[pl.ds(0, channels)], small_sems.at[0]),
        pltpu.make_async_copy(
            weight_own, weight_twice.at[pl.ds(channels, channels)], small_sems.at[1]
        ),
        pltpu.make_async_copy(latent_hbm, latent_buf, small_sems.at[2]),
    ]

    own_copies = [
        pltpu.make_async_copy(sources[which], own.at[which], own_sems.at[which])
        for which in range(3)
    ]
    for copy in own_copies:
        copy.start()

    count = jnp.max(dest_ref[...].astype(jnp.float32), axis=1, keepdims=True) + 1.0
    count_pair[0] = jnp.broadcast_to(count, (videos, 128)).astype(jnp.int32)
    for copy in own_copies:
        copy.wait()

    def lay(head):
        for which in range(3):
            column = head * HD if isinstance(head, int) else pl.multiple_of(head * HD, HD)
            laid[head, which] = own[which, :, pl.ds(column, HD)]

    sweep(0, columns // HD, lay, 32)

    pl.semaphore_wait(barrier, half)

    partner_copy = pltpu.make_async_remote_copy(
        src_ref=count_pair.at[0],
        dst_ref=count_pair.at[1],
        send_sem=send_sems.at[0],
        recv_sem=pair_recv,
        device_id={"seq": partner},
        device_id_type=MESH,
    )
    partner_copy.start()

    def send_count(p):
        pltpu.make_async_remote_copy(
            src_ref=count_pair,
            dst_ref=count_buf.at[rank],
            send_sem=send_sems.at[3],
            recv_sem=part_recv.at[0],
            device_id={"seq": base + (rank + p) % half},
            device_id_type=MESH,
        ).start()

    for item in range(items):

        def send_heads(p):
            peer = (rank + p) % half
            pltpu.make_async_remote_copy(
                src_ref=laid.at[peer * items + item],
                dst_ref=heads_buf.at[item, rank],
                send_sem=send_sems.at[1],
                recv_sem=head_recv.at[item],
                device_id={"seq": base + peer},
                device_id_type=MESH,
            ).start()

        sweep(1, half, send_heads)

        if item == 0:
            partner_copy.wait()
            pltpu.make_async_copy(count_pair, count_buf.at[rank], part_recv.at[0]).start()
            sweep(1, half, send_count)

    for item in range(items):
        pltpu.make_async_copy(
            laid.at[rank * items + item], heads_buf.at[item, rank], head_recv.at[item]
        ).start()
    for copy in small_copies:
        copy.start()

    def vouch(p):
        pl.semaphore_signal(
            vouched,
            inc=1,
            device_id={"seq": base + (rank + p) % half},
            device_id_type=MESH,
        )

    sweep(1, half, vouch)

    for copy in small_copies:
        copy.wait()
    weight_rows[...] = weight_twice[...].astype(jnp.float32).T.astype(jnp.bfloat16)

    tokens = latent_buf.shape[1]
    slot_hots, latent_means, shares = [], [], []
    for v in range(videos):
        hot = lax.broadcasted_iota(jnp.int32, (cap, tokens), 0) == dest_ref[v : v + 1, :]
        hot = hot.astype(jnp.float32)
        latent_sum = jnp.dot(
            hot,
            latent_buf[v],
            precision=lax.Precision.HIGHEST,
            preferred_element_type=jnp.float32,
        )
        tally = jnp.sum(hot, axis=1, keepdims=True)
        inverse = 1.0 / jnp.maximum(tally, 1.0)
        slot_hots.append(jnp.concatenate([hot.T] * 3, axis=1).astype(jnp.bfloat16))
        latent_means.append(latent_sum * inverse)
        shares.append(tally * inverse)

    pltpu.make_async_copy(count_buf, count_buf, part_recv.at[0]).wait()
    video = (rank * items) // HEADS
    lane = lax.broadcasted_iota(jnp.int32, (1, keys_total), 1)
    group_of = ((lane % rows) // cap) * half + lane // rows
    place_of = lane % cap

    def count_step(r, held):
        pair = count_buf[r]
        for side in range(2):
            row = pair[side, 0:1]
            for v in range(1, videos):
                row = jnp.where(video == v, pair[side, v : v + 1], row)
            wide = jnp.concatenate([row] * (keys_total // 128), axis=1)
            owner = (side * half + base) % n + r
            held = jnp.where(group_of == owner, wide, held)
        return held

    held = jnp.zeros((1, keys_total), jnp.int32)
    if half <= 16:
        for r in range(half):
            held = count_step(r, held)
    else:
        held = lax.fori_loop(0, half, count_step, held)
    live = place_of < held

    def by_blocks(block, body):
        if keys_total <= 4 * block:
            for index in range(keys_total // block):
                body(index)
        else:

            def step(index, carry):
                body(index)
                return carry

            lax.fori_loop(0, keys_total // block, step, 0)

    left = lax.broadcasted_iota(jnp.int32, (cap // 2, 2 * channels), 1) < channels

    together = 2 if items % 2 == 0 else 1
    block = min(keys_total, 256)
    ranks = block // rows
    for first in range(0, items, together):
        heads = range(first, first + together)
        for item in heads:
            pltpu.make_async_copy(
                heads_buf.at[item], heads_buf.at[item], head_recv.at[item]
            ).wait()

        def attend(index):
            at = pl.ds(pl.multiple_of(index * block, block), block)
            scores = [
                lax.dot_general(
                    heads_buf[item, pl.ds(index * ranks, ranks), 0].reshape(block, HD),
                    heads_buf[item, :, 1].reshape(keys_total, HD),
                    (((1,), (1,)), ((), ())),
                    preferred_element_type=jnp.float32,
                )
                * scale
                for item in heads
            ]
            scores = [jnp.where(live, s, NEG_BIG) for s in scores]
            weights = [jnp.exp(s - jnp.max(s, axis=-1, keepdims=True)) for s in scores]
            probs = [
                (w * (1.0 / jnp.sum(w, axis=-1, keepdims=True))).astype(jnp.bfloat16)
                for w in weights
            ]
            attended = [
                jnp.dot(
                    p,
                    heads_buf[item, :, 2].reshape(keys_total, HD),
                    preferred_element_type=jnp.float32,
                ).astype(jnp.bfloat16)
                for p, item in zip(probs, heads)
            ]
            term = jnp.dot(
                jnp.concatenate(attended, axis=1),
                weight_rows[first * HD : (first + together) * HD, :],
                preferred_element_type=jnp.float32,
            )
            if first == 0:
                total[at, :] = term
            else:
                total[at, :] += term

        by_blocks(block, attend)

    both = total[...].reshape(half, 2, 2, cap // 2, 2 * channels)
    stage[...] = jnp.where(left, both[:, :, 0], both[:, :, 1])

    pl.semaphore_wait(vouched, half - 1)

    def send_part(side, peer):
        pltpu.make_async_remote_copy(
            src_ref=stage.at[peer, side],
            dst_ref=parts.at[me],
            send_sem=send_sems.at[2],
            recv_sem=part_recv.at[1],
            device_id={"seq": side * half + peer},
            device_id_type=MESH,
        ).start()

    sweep(0, half, lambda p: send_part(1 - branch, (rank + p) % half))
    sweep(1, half, lambda p: send_part(branch, (rank + p) % half))
    pltpu.make_async_copy(stage.at[rank, branch], parts.at[me], part_recv.at[1]).start()
    pltpu.make_async_copy(parts, parts, part_recv.at[1]).wait()

    span = half // videos
    for v in range(videos):
        cond = jnp.sum(parts[v * span : (v + 1) * span], axis=0)
        uncond = jnp.sum(parts[half + v * span : half + (v + 1) * span], axis=0)
        merged = jnp.concatenate(
            [
                jnp.where(left, cond, pltpu.roll(uncond, channels, 1)),
                jnp.where(left, pltpu.roll(cond, channels, 1), uncond),
            ],
            axis=0,
        )
        terms, rest = [], merged
        for _ in range(3):
            terms.append(rest.astype(jnp.bfloat16))
            rest = rest - terms[-1].astype(jnp.float32)
        velocity = jnp.dot(
            slot_hots[v],
            jnp.concatenate(terms, axis=0),
            preferred_element_type=jnp.float32,
        )
        velocity_ref[0, v] = velocity[:, :channels]
        velocity_ref[1, v] = velocity[:, channels:]
        merged = shares[v] * merged
        slot_ref[0, v] = merged[:, :channels]
        slot_ref[1, v] = merged[:, channels:]
        slot_ref[2, v] = latent_means[v]

    pltpu.make_async_copy(
        count_buf.at[pl.ds(0, half - 1)], count_buf.at[pl.ds(0, half - 1)], send_sems.at[3]
    ).wait()
    sent = heads_buf.at[:, pl.ds(0, half - 1)]
    pltpu.make_async_copy(sent, sent, send_sems.at[1]).wait()
    pltpu.make_async_copy(
        parts.at[pl.ds(0, n - 1)], parts.at[pl.ds(0, n - 1)], send_sems.at[2]
    ).wait()


def local(
    queries, keys, values, live_counts, merge_dest, latents, guidance, step_index, out_weight
):
    n = lax.axis_size("seq")
    half = n // 2
    rows, columns = queries.shape
    videos, tokens, channels = latents.shape
    items = columns // HD // half
    cap = rows // 2
    outside = pl.BlockSpec(memory_space=pltpu.HBM)
    inside = pl.BlockSpec(memory_space=pltpu.VMEM)
    velocities, slots = pl.pallas_call(
        functools.partial(kernel, n, items, videos),
        out_shape=(
            jax.ShapeDtypeStruct((2, videos, tokens, channels), jnp.float32),
            jax.ShapeDtypeStruct((3, videos, cap, channels), jnp.float32),
        ),
        in_specs=[outside] * 3 + [inside] + [outside] * 2,
        out_specs=(inside, inside),
        scratch_shapes=[
            pltpu.VMEM((items, half, 3, rows, HD), jnp.bfloat16),
            pltpu.VMEM((3, rows, columns), jnp.bfloat16),
            pltpu.VMEM((columns // HD, 3, rows, HD), jnp.bfloat16),
            pltpu.VMEM((2, videos, 128), jnp.int32),
            pltpu.VMEM((half, 2, videos, 128), jnp.int32),
            pltpu.VMEM((2 * channels, items * HD), jnp.bfloat16),
            pltpu.VMEM((items * HD, 2 * channels), jnp.bfloat16),
            pltpu.VMEM((videos, tokens, channels), jnp.float32),
            pltpu.VMEM((half * rows, 2 * channels), jnp.float32),
            pltpu.VMEM((half, 2, cap // 2, 2 * channels), jnp.float32),
            pltpu.VMEM((n, cap // 2, 2 * channels), jnp.float32),
            pltpu.SemaphoreType.DMA((2,)),
            pltpu.SemaphoreType.DMA((3,)),
            pltpu.SemaphoreType.DMA((items,)),
            pltpu.SemaphoreType.DMA((4,)),
            pltpu.SemaphoreType.DMA((3,)),
            pltpu.SemaphoreType.DMA,
            pltpu.SemaphoreType.REGULAR,
        ],
        compiler_params=pltpu.CompilerParams(
            collective_id=0, has_side_effects=True, vmem_limit_bytes=55040 * 1024
        ),
    )(
        queries,
        keys,
        values,
        merge_dest,
        latents,
        out_weight.T,
    )
    step_value = step_index.astype(jnp.float32)
    sigma_now = sigma_of(step_value)
    sigma_next = sigma_of(step_value + float(STRIDE))
    gain = guidance[:, None, None]
    velocity = velocities[1] + gain * (velocities[0] - velocities[1])
    denoised = latents - sigma_now[:, None, None] * velocity
    merged = slots[1] + gain * (slots[0] - slots[1])
    merged_next = slots[2] + (sigma_next - sigma_now)[:, None, None] * merged
    return denoised, merged_next


def solution(mesh):
    placed = (
        P(("jobs", "seq"), None),
        P(("jobs", "seq"), None),
        P(("jobs", "seq"), None),
        P("jobs", "seq"),
        P("jobs", "seq"),
        P("jobs", "seq", None),
        P("jobs"),
        P("jobs"),
        P(),
    )
    return jax.shard_map(
        local,
        mesh=mesh,
        in_specs=placed,
        out_specs=(P("jobs", "seq", None), P("jobs", "seq", None)),
        check_vma=False,
    )
```
